256 devices in a mesh: dp: 32 (over z_lo, x, core), tile: 8 (over z_hi, y).
Axes of the slice: x: 4, y: 4, z: 8 (z_hi: 2, z_lo: 4; z = z_hi * 4 + z_lo), core: 2. Of those that a mesh axis runs over, the one named last changes fastest.
Arguments:
- features: bfloat16 [32, 40960, 256], P('dp', 'tile'), may hold values from -6 to 6
- kernels: bfloat16 [32, 100, 256], P('dp'), may hold values from -0.375 to 0.375
- cotangent: bfloat16 [32, 100, 40960], P('dp', None, 'tile'), may hold values from -6 to 6
- w_feat_gate: bfloat16 [256, 256], replicated, may hold values from -0.375 to 0.375
- w_value: bfloat16 [256, 256], replicated, may hold values from -0.375 to 0.375
- w_up: bfloat16 [256, 2048], replicated, may hold values from -0.375 to 0.375
- w_down: bfloat16 [2048, 256], replicated, may hold values from -0.125 to 0.125
Outputs:
- grad_features: float32 [32, 40960, 256], P('dp', 'tile')
- grad_kernels: float32 [32, 100, 256], P('dp')
- grad_feat_gate: float32 [256, 256], replicated
- grad_value: float32 [256, 256], replicated
- grad_up: float32 [256, 2048], replicated
- grad_down: float32 [2048, 256], replicated
The draws below stay inside these ranges and needn't reach their ends.
All inputs are finite; a program needn't handle non-finite values.
Results may differ from the reference program's by a relative error of at most 0.0034.
Values sent between devices are 32-bit elements; how exact they have to be, the bound alone decides.
A program may use at most 128 MiB of HBM per device.

```python
import jax
import jax.numpy as jnp
from jax import lax

N = 100
C = 256
FF = 2048
CELLS = 40960
FRAMES = 32


def block_scale(rng, shape, cuts, smallest, high):
    gain, own = 1.0, jax.random.fold_in(rng, 6)
    for position, shards_of in cuts:
        heights = jnp.exp(jax.random.uniform(jax.random.fold_in(own, position), (shards_of,), jnp.float32, smallest / len(cuts), high / len(cuts)))
        gain = gain * jnp.repeat(heights, shape[position] // shards_of).reshape([-1 if axis == position else 1 for axis in range(len(shape))])
    return gain


def normal_values(own_key, extent, spread, limit, pieces=(), dtype=jnp.bfloat16):
    result = jax.random.normal(own_key, extent, jnp.float32) * spread
    if len(pieces) > 0:
        result = block_scale(own_key, extent, pieces, -0.22, 0.18) * result
    return jnp.clip(result, min=-limit, max=limit).astype(dtype)


def setup_inputs(seed: int = 0) -> dict:
    seeds = jax.random.split(jax.random.key(seed), 8)
    return {
        "features": normal_values(seeds[0], (FRAMES, CELLS, C), 1.0, 6.0, ((0, 32), (1, 8))),
        "kernels": normal_values(seeds[1], (FRAMES, N, C), C ** -0.5, 0.375, ((0, 32),)),
        "cotangent": normal_values(seeds[2], (FRAMES, N, CELLS), 1.0, 6.0, ((0, 32), (2, 8))),
        "w_feat_gate": normal_values(seeds[3], (C, C), C ** -0.5, 0.375),
        "w_value": normal_values(seeds[4], (C, C), C ** -0.5, 0.375),
        "w_up": normal_values(seeds[5], (C, FF), C ** -0.5, 0.375),
        "w_down": normal_values(seeds[6], (FF, C), FF ** -0.5, 0.125),
    }


def normalize(values):
    mean = lax.optimization_barrier(jnp.mean(values, axis=-1, keepdims=True))
    centred = values - mean
    variance = lax.optimization_barrier(jnp.mean(centred * centred, axis=-1, keepdims=True))
    return centred * lax.rsqrt(variance + 1e-05)

def head(pooled, kern, w_fg, w_val, w_upper, w_lower):
    top = lax.Precision.HIGHEST
    gate_f = jax.nn.sigmoid(jnp.dot(pooled, w_fg, precision=top))
    value = jnp.dot(pooled, w_val, precision=top)
    first = normalize(gate_f * value + kern)
    hidden = jax.nn.gelu(jnp.dot(first, w_upper, precision=top), approximate=True)
    return normalize(first + jnp.dot(hidden, w_lower, precision=top))

def frame_grads(feat, kern, cot, weights32):
    scale = 1.0 / jnp.sqrt(jnp.float32(CELLS))
    logits = jnp.dot(kern, feat.T, preferred_element_type=jnp.float32)
    prob = jax.nn.sigmoid(logits)
    prob_b = prob.astype(jnp.bfloat16)
    pooled = jnp.dot(prob_b, feat, preferred_element_type=jnp.float32) * scale
    kern32 = kern.astype(jnp.float32)
    newk, pull = jax.vjp(head, pooled, kern32, *weights32)
    newk_b = newk.astype(jnp.bfloat16)
    dnew = jnp.dot(cot, feat, preferred_element_type=jnp.float32)
    grads = pull(dnew)
    d_pooled, d_headk = (grads[0], grads[1])
    d_scaled = (d_pooled * scale).astype(jnp.bfloat16)
    d_prob = jnp.dot(d_scaled, feat.T, preferred_element_type=jnp.float32)
    d_logits = (d_prob * prob * (1.0 - prob)).astype(jnp.bfloat16)
    grad_k = d_headk + jnp.dot(d_logits, feat, preferred_element_type=jnp.float32)
    grad_f = jnp.dot(cot.T, newk_b, preferred_element_type=jnp.float32) + jnp.dot(prob_b.T, d_scaled, preferred_element_type=jnp.float32) + jnp.dot(d_logits.T, kern, preferred_element_type=jnp.float32)
    return (grad_f, grad_k, tuple(grads[2:]))

def reference(features, kernels, cotangent, w_feat_gate, w_value, w_up, w_down):
    weights32 = tuple((w.astype(jnp.float32) for w in (w_feat_gate, w_value, w_up, w_down)))

    def step(carry, items):
        feat, kern, cot = items
        grad_f, grad_k, terms = frame_grads(feat, kern, cot, weights32)
        carry = tuple((a + b for a, b in zip(carry, terms)))
        return (carry, (grad_f, grad_k))
    start = tuple((jnp.zeros(w.shape, jnp.float32) for w in weights32))
    totals, (grad_features, grad_kernels) = lax.scan(step, start, (features, kernels, cotangent))
    return (grad_features, grad_kernels, totals[0], totals[1], totals[2], totals[3])
```

```python
import functools
import math

import jax
import jax.numpy as jnp
from jax import lax
from jax.experimental import pallas as pl
from jax.experimental.pallas import tpu as pltpu
from jax.sharding import PartitionSpec as P

MESH = pl.DeviceIdType.MESH
F32, BF16 = jnp.float32, jnp.bfloat16
X, Y, ZL, ZH = 4, 4, 4, 2
ROWS = 112
PART = 56
CHUNK = 1024
PIECE = 40
BLOCK = ZL * PIECE
SLICE = X * BLOCK
NT = (((1,), (1,)), ((), ()))
NN = (((1,), (0,)), ((), ()))
TN = (((0,), (0,)), ((), ()))


def split(v):
    hi = v.astype(BF16)
    return hi, (v - hi.astype(F32)).astype(BF16)


def dot2(stacked, w, dims):
    both = lax.dot_general(stacked, w, dims, preferred_element_type=F32)
    return both[:ROWS] + both[ROWS:]


def stack(v):
    return jnp.concatenate(split(v), axis=0)


def outer3(a, b):
    ah, al = split(a)
    bh, bl = split(b)
    return lax.dot_general(
        jnp.concatenate([ah, ah, al], axis=0),
        jnp.concatenate([bh, bl, bh], axis=0),
        TN,
        preferred_element_type=F32,
    )


def mean(v):
    return jnp.mean(v, axis=-1, keepdims=True)


def norm(v):
    c = v - mean(v)
    r = lax.rsqrt(mean(c * c) + 1e-05)
    return c * r, r


def norm_back(dy, y, r):
    return r * (dy - mean(dy) - y * mean(dy * y))


def place(ref, v):
    for h in range(2):
        for r in range(2):
            ref[2 * h + r] = v[r * PART : (r + 1) * PART, h * 128 : (h + 1) * 128]


def whole(ref):
    return jnp.concatenate(
        [jnp.concatenate([ref[2 * h], ref[2 * h + 1]], axis=0) for h in range(2)], axis=1
    )


class Place:
    def __init__(self):
        dp, tile = lax.axis_index("dp"), lax.axis_index("tile")
        self.tile = tile
        self.c = lax.rem(dp, 2)
        self.x = lax.rem(dp // 2, X)
        self.zl = dp // (2 * X)
        self.y = lax.rem(tile, Y)
        self.zh = tile // Y

    def at(self, dx=0, dy=0, dzl=0, dzh=0, dc=0):
        x = lax.rem(self.x + dx, X)
        y = lax.rem(self.y + dy, Y)
        zl = lax.rem(self.zl + dzl, ZL)
        zh = lax.rem(self.zh + dzh, ZH)
        c = lax.rem(self.c + dc, 2)
        return ((zl * X + x) * 2 + c, zh * Y + y)


class Sems:
    def __init__(self, send, recv):
        self.send, self.recv, self.n = send, recv, 0

    def copy(self, src, dst, device):
        i = self.n
        self.n += 1
        return pltpu.make_async_remote_copy(
            src_ref=src,
            dst_ref=dst,
            send_sem=self.send.at[i],
            recv_sem=self.recv.at[i],
            device_id=device,
            device_id_type=MESH,
        )


class TileSum:
    def __init__(self, me, sems, mine, got, pair, total):
        self.me, self.sems = me, sems
        self.mine, self.got, self.pair, self.total = mine, got, pair, total
        self.all = []

    def start(self, copies):
        for c in copies:
            c.start()
        self.all += copies
        return copies

    def scatter(self):
        me = self.me
        self.a = self.start(
            [
                self.sems.copy(self.mine.at[lax.rem(me.y + d, Y)], self.got.at[d - 1], me.at(dy=d))
                for d in (1, 2, 3)
            ]
        )

    def exchange(self):
        for c in self.a:
            c.wait_recv()
        me = self.me
        self.pair[0] = (self.mine[me.y] + self.got[0]) + (self.got[1] + self.got[2])
        self.b = self.start([self.sems.copy(self.pair.at[0], self.pair.at[1], me.at(dzh=1))])

    def gather(self):
        self.b[0].wait_recv()
        me = self.me
        self.total[me.y] = self.pair[0] + self.pair[1]
        here = self.total.at[me.y]
        self.d = self.start([self.sems.copy(here, here, me.at(dy=d)) for d in (1, 2, 3)])

    def result(self):
        for c in self.d:
            c.wait_recv()
        return whole(self.total)

    def close(self):
        for c in self.all:
            c.wait_send()


def section(
    scale,
    feat_in,
    kern_in,
    cot_in,
    wfg_in,
    wval_in,
    wup_in,
    wdown_in,
    gathered,
    prob_out,
    dlog_out,
    newk_out,
    dscaled_out,
    gk_out,
    feat,
    cot,
    prob,
    prob_b,
    dlog,
    wfg,
    wval,
    wup,
    wdown,
    acc,
    hid,
    slope,
    dhid,
    tmp,
    sums,
    got,
    pair,
    total,
    terms,
    r0,
    mine,
    r1,
    half,
    r2,
    local,
    send,
    recv,
):
    me = Place()
    sems = Sems(send, recv)
    n = kern_in.shape[0]
    cells = feat_in.shape[0]
    chunks = cells // CHUNK
    ff = wup_in.shape[1] // 256
    c, x, y, zl, zh = me.c, me.x, me.y, me.zl, me.zh

    def part(i):
        return pl.ds(pl.multiple_of(i * CHUNK, CHUNK), CHUNK)

    def feat_copy(i):
        return pltpu.make_async_copy(feat_in.at[part(i), :], feat.at[part(i), :], local.at[i])

    def cot_copy(i):
        return pltpu.make_async_copy(cot_in.at[:, part(i)], cot.at[:, part(i)], local.at[chunks + i])

    for i in range(chunks):
        feat_copy(i).start()
    for i in range(chunks):
        cot_copy(i).start()
    base = 2 * chunks
    weights = [
        pltpu.make_async_copy(a, b, local.at[base + i])
        for i, (a, b) in enumerate(((wfg_in, wfg), (wval_in, wval), (wup_in, wup), (wdown_in, wdown)))
    ]
    for w in weights:
        w.start()
    base += 4

    partners = [me.at(dc=1)]
    partners += [me.at(dy=d) for d in (1, 2, 3)]
    partners += [me.at(dx=d) for d in (1, 2, 3)]
    partners += [me.at(dzl=d % ZL, dzh=d // ZL) for d in range(1, ZL * ZH)]
    barrier = pltpu.get_barrier_semaphore()
    for p in partners:
        pl.semaphore_signal(barrier, inc=1, device_id=p, device_id_type=MESH)

    kern = kern_in[...]

    acc[...] = jnp.zeros_like(acc)

    def pool(i, carry):
        feat_copy(i).wait()
        f = feat[part(i), :]
        p = jax.nn.sigmoid(lax.dot_general(kern, f, NT, preferred_element_type=F32))
        prob[:, part(i)] = p
        pb = p.astype(BF16)
        prob_b[:, part(i)] = pb
        acc[:n, :] += jnp.dot(pb, f, preferred_element_type=F32)
        return carry

    lax.fori_loop(0, chunks, pool, 0)
    sum_p = TileSum(me, sems, sums.at[0], got.at[0], pair.at[0], total.at[0])
    sum_d = TileSum(me, sems, sums.at[1], got.at[1], pair.at[1], total.at[1])
    sum_m = TileSum(me, sems, sums.at[2], got.at[2], pair.at[2], total.at[2])
    place(sums.at[0], acc[...])
    pl.semaphore_wait(barrier, len(partners))
    sum_p.scatter()

    prob_copy = pltpu.make_async_copy(prob_b, prob_out, local.at[base])
    prob_copy.start()

    acc[...] = jnp.zeros_like(acc)

    def new(i, carry):
        cot_copy(i).wait()
        acc[:n, :] += jnp.dot(cot[:, part(i)], feat[part(i), :], preferred_element_type=F32)
        return carry

    lax.fori_loop(0, chunks, new, 0)
    place(sums.at[1], acc[...])
    sum_d.scatter()
    sum_p.exchange()
    sum_d.exchange()
    for w in weights:
        w.wait()
    acc[...] = jnp.zeros_like(acc)
    acc[:n, :] = kern.astype(F32)
    kern32 = acc[...]
    sum_p.gather()
    sum_d.gather()

    pooled = sum_p.result() * scale
    pooled2 = stack(pooled)
    gate = jax.nn.sigmoid(dot2(pooled2, wfg[...], NN))
    value = dot2(pooled2, wval[...], NN)
    k1, rs1 = norm(gate * value + kern32)
    k1s = stack(k1)
    z = k1
    for j in range(ff):
        a = dot2(k1s, wup[:, j * 256 : (j + 1) * 256], NN)
        t = jnp.tanh(0.7978845608028654 * (a + 0.044715 * (a * a * a)))
        up = 0.5 * (1.0 + t)
        h = a * up
        hid[j] = h
        slope[j] = up + 0.5 * a * (1.0 - t * t) * (0.7978845608028654 * (1.0 + 0.134145 * (a * a)))
        z = z + dot2(stack(h), wdown[j * 256 : (j + 1) * 256, :], NN)
    k3, rs3 = norm(z)
    newk_out[...] = k3.astype(BF16)

    dz = norm_back(sum_d.result(), k3, rs3)
    dzs = stack(dz)
    dk1 = dz
    for j in range(ff):
        da = dot2(dzs, wdown[j * 256 : (j + 1) * 256, :], NT) * slope[j]
        dhid[j] = da
        dk1 = dk1 + dot2(stack(da), wup[:, j * 256 : (j + 1) * 256], NT)
    du = norm_back(dk1, k1, rs1)
    dgate = du * value * (gate * (1.0 - gate))
    dvalue = du * gate
    dpooled = dot2(stack(dgate), wfg[...], NT) + dot2(stack(dvalue), wval[...], NT)
    dscaled = (dpooled * scale).astype(BF16)
    dscaled_out[...] = dscaled
    acc[...] = du

    up_term = outer3(k1, dhid[me.tile])
    down_term = outer3(hid[me.tile], dz)
    tmp[0] = outer3(pooled, dgate)
    tmp[1] = outer3(pooled, dvalue)
    own = pl.ds(pl.multiple_of(me.tile * 32, 32), 32)
    for h in range(2):
        lanes = slice(h * 128, (h + 1) * 128)
        terms[h, :256, :] = up_term[:, lanes]
        terms[h, 256:512, :] = down_term[:, lanes]
        terms[h, 512:544, :] = tmp[0, own, lanes]
        terms[h, 544:576, :] = tmp[1, own, lanes]
        terms[h, 576:, :] = jnp.zeros((SLICE - 576, 128), F32)
    c0 = sems.copy(terms.at[1 - c], r0, me.at(dc=1))
    c0.start()

    ds = dscaled[:n]
    sums[2] = jnp.zeros_like(sums[2])

    def mask(i, carry):
        f = feat[part(i), :]
        p = prob[:, part(i)]
        dp = lax.dot_general(ds, f, NT, preferred_element_type=F32)
        dl = (dp * p * (1.0 - p)).astype(BF16)
        dlog[:, part(i)] = dl
        return carry + jnp.dot(dl, f, preferred_element_type=F32)

    macc = lax.fori_loop(0, 2, mask, jnp.zeros((n, 256), F32))
    c0.wait_recv()
    mine[...] = terms[c] + r0[...]

    def rows(i, size):
        return pl.ds(pl.multiple_of(i * size, size), size)

    c1 = [
        sems.copy(mine.at[rows(lax.rem(x + d, X), BLOCK), :], r1.at[d - 1], me.at(dx=d)) for d in (1, 2, 3)
    ]
    for cp in c1:
        cp.start()
    macc = lax.fori_loop(2, chunks, mask, macc)
    dlog_copy = pltpu.make_async_copy(dlog, dlog_out, local.at[base + 1])
    dlog_copy.start()
    gk_out[...] = jnp.zeros_like(gk_out)
    gk_out[:n, :] = macc
    place(sums.at[2], gk_out[...])
    sum_m.scatter()
    for cp in c1:
        cp.wait_recv()
    half[...] = (mine[rows(x, BLOCK), :] + r1[0]) + (r1[1] + r1[2])
    c2 = [
        sems.copy(half.at[rows(lax.rem(zl + d, ZL), PIECE), :], r2.at[d - 1], me.at(dzl=d)) for d in (1, 2, 3)
    ]
    for cp in c2:
        cp.start()
    sum_m.exchange()
    for cp in c2:
        cp.wait_recv()

    spot = rows(x * ZL + zl, PIECE)
    gathered[c, zh, y, spot, :] = (half[rows(zl, PIECE), :] + r2[0]) + (r2[1] + r2[2])
    here = gathered.at[c, zh, y, spot, :]
    cz = [sems.copy(here, here, me.at(dzl=d % ZL, dzh=d // ZL)) for d in range(1, ZL * ZH)]
    for cp in cz:
        cp.start()
    sum_m.gather()
    for cp in cz:
        cp.wait_recv()

    def block(bx, by):
        return gathered.at[c, :, by, rows(bx, BLOCK), :]

    mx, my = 1 - c, c
    started = []

    def send_to(b, **where):
        cp = sems.copy(b, b, me.at(**where))
        cp.start()
        started.append(cp)
        return cp

    first = block(x, y)
    mid = [send_to(first, dx=mx * d, dy=my * d) for d in (1, 3, 2)]
    last = [[send_to(first, dx=my * d, dy=mx * d) for d in (1, 3, 2)]]
    twin = [send_to(first, dc=1)]
    for d, cp in zip((1, 3, 2), mid):
        cp.wait_recv()
        b = block(lax.rem(x + mx * (4 - d), X), lax.rem(y + my * (4 - d), Y))
        last.append([send_to(b, dx=my * e, dy=mx * e) for e in (1, 3, 2)])
        twin.append(send_to(b, dc=1))
    gk_out[...] = sum_m.result() + acc[...]
    for d, group in zip((0, 1, 3, 2), last):
        for e, cp in zip((1, 3, 2), group):
            cp.wait_recv()
            bx = lax.rem(x + mx * (4 - d) + my * (4 - e), X)
            by = lax.rem(y + my * (4 - d) + mx * (4 - e), Y)
            twin.append(send_to(block(bx, by), dc=1))
    for cp in twin:
        cp.wait_recv()

    for s in (sum_p, sum_d, sum_m):
        s.close()
    for cp in [c0] + c1 + c2 + cz + started:
        cp.wait_send()
    prob_copy.wait()
    dlog_copy.wait()


def finish(
    gathered, cot, prob_b, dlog, newk, dscaled, kern, grad_f, g_gate, g_value, g_up, g_down, sem
):
    n = kern.shape[0]
    copies = []
    for h in range(2):
        lanes = pl.ds(h * 128, 128)
        for t in range(ZH * Y):
            src = gathered.at[h, t // Y, t % Y]
            pairs = (
                (src.at[0:256, :], g_up.at[:, pl.ds(t * 256 + h * 128, 128)]),
                (src.at[256:512, :], g_down.at[pl.ds(t * 256, 256), lanes]),
                (src.at[512:544, :], g_gate.at[pl.ds(t * 32, 32), lanes]),
                (src.at[544:576, :], g_value.at[pl.ds(t * 32, 32), lanes]),
            )
            for a, b in pairs:
                copies.append(pltpu.make_async_copy(a, b, sem.at[len(copies)]))

    @pl.when(pl.program_id(0) == 0)
    def _():
        for cp in copies:
            cp.start()

    def term(a, b):
        return lax.dot_general(a, b, TN, preferred_element_type=F32)

    grad_f[...] = term(cot[...], newk[:n, :]) + term(prob_b[...], dscaled[:n, :]) + term(dlog[...], kern[...])

    @pl.when(pl.program_id(0) == pl.num_programs(0) - 1)
    def _():
        for cp in copies:
            cp.wait()


def shards(features, kernels, cotangent, w_feat_gate, w_value, w_up, w_down):
    feat, kern, cot = features[0], kernels[0], cotangent[0]
    n, channels = kern.shape
    cells = feat.shape[0]
    chunks = cells // CHUNK
    ff = w_up.shape[1] // 256
    scale = 1.0 / math.sqrt(lax.axis_size("tile") * cells)
    anywhere = pl.BlockSpec(memory_space=pl.ANY)
    vmem = pl.BlockSpec(memory_space=pltpu.VMEM)
    copies = 64
    shape = jax.ShapeDtypeStruct
    gathered, prob_b, dlog, newk, dscaled, gk = pl.pallas_call(
        functools.partial(section, scale),
        out_shape=(
            shape((2, ZH, Y, SLICE, 128), F32),
            shape((n, cells), BF16),
            shape((n, cells), BF16),
            shape((ROWS, channels), BF16),
            shape((ROWS, channels), BF16),
            shape((ROWS, channels), F32),
        ),
        in_specs=[anywhere, vmem, anywhere, anywhere, anywhere, anywhere, anywhere],
        out_specs=(vmem, anywhere, anywhere, vmem, vmem, vmem),
        scratch_shapes=[
            pltpu.VMEM((cells, channels), BF16),
            pltpu.VMEM((n, cells), BF16),
            pltpu.VMEM((n, cells), F32),
            pltpu.VMEM((n, cells), BF16),
            pltpu.VMEM((n, cells), BF16),
            pltpu.VMEM(w_feat_gate.shape, BF16),
            pltpu.VMEM(w_value.shape, BF16),
            pltpu.VMEM(w_up.shape, BF16),
            pltpu.VMEM(w_down.shape, BF16),
            pltpu.VMEM((ROWS, channels), F32),
            pltpu.VMEM((ff, ROWS, 256), F32),
            pltpu.VMEM((ff, ROWS, 256), F32),
            pltpu.VMEM((ff, ROWS, 256), F32),
            pltpu.VMEM((2, 256, 256), F32),
            pltpu.VMEM((3, 4, PART, 128), F32),
            pltpu.VMEM((3, 3, PART, 128), F32),
            pltpu.VMEM((3, 2, PART, 128), F32),
            pltpu.VMEM((3, 4, PART, 128), F32),
            pltpu.VMEM((2, SLICE, 128), F32),
            pltpu.VMEM((SLICE, 128), F32),
            pltpu.VMEM((SLICE, 128), F32),
            pltpu.VMEM((3, BLOCK, 128), F32),
            pltpu.VMEM((BLOCK, 128), F32),
            pltpu.VMEM((3, PIECE, 128), F32),
            pltpu.SemaphoreType.DMA((2 * chunks + 6,)),
            pltpu.SemaphoreType.DMA((copies + 8,)),
            pltpu.SemaphoreType.DMA((copies + 8,)),
        ],
        compiler_params=pltpu.CompilerParams(
            collective_id=0, has_side_effects=True, vmem_limit_bytes=40 * 2**20
        ),
        name="section",
    )(feat, kern, cot, w_feat_gate, w_value, w_up, w_down)

    wide = pl.BlockSpec((n, CHUNK), lambda i: (0, i))
    grad_f, g_gate, g_value, g_up, g_down = pl.pallas_call(
        finish,
        grid=(chunks,),
        out_shape=(
            shape((cells, channels), F32),
            shape(w_feat_gate.shape, F32),
            shape(w_value.shape, F32),
            shape(w_up.shape, F32),
            shape(w_down.shape, F32),
        ),
        in_specs=[anywhere, wide, wide, wide, vmem, vmem, vmem],
        out_specs=(
            pl.BlockSpec((CHUNK, channels), lambda i: (i, 0)),
            anywhere,
            anywhere,
            anywhere,
            anywhere,
        ),
        scratch_shapes=[pltpu.SemaphoreType.DMA((ZH * Y * 2 * 4,))],
        compiler_params=pltpu.CompilerParams(vmem_limit_bytes=24 * 2**20),
        name="finish",
    )(gathered, cot, prob_b, dlog, newk, dscaled, kern)
    return (grad_f[None], gk[None, :n], g_gate, g_value, g_up, g_down)


def solution(mesh):
    placed = (P("dp", "tile", None), P("dp", None, None), P("dp", None, "tile"), P(), P(), P(), P())
    return jax.shard_map(
        shards,
        mesh=mesh,
        in_specs=placed,
        out_specs=(P("dp", "tile", None), P("dp", None, None), P(), P(), P(), P()),
        check_vma=False,
    )
```

```python
import functools
import math

import jax
import jax.numpy as jnp
from jax import lax
from jax.experimental import pallas as pl
from jax.experimental.pallas import tpu as pltpu
from jax.sharding import PartitionSpec as P

MESH = pl.DeviceIdType.MESH
F32, BF16 = jnp.float32, jnp.bfloat16
X, Y, ZL, ZH = 4, 4, 4, 2
ROWS = 112
PART = 56
CHUNK = 1024
PIECE = 32
SMALL = 16
BLOCK = ZL * PIECE + SMALL
NT = (((1,), (1,)), ((), ()))
NN = (((1,), (0,)), ((), ()))
TN = (((0,), (0,)), ((), ()))


def split(v):
    hi = v.astype(BF16)
    return hi, (v - hi.astype(F32)).astype(BF16)


def dot2(stacked, w, dims):
    both = lax.dot_general(stacked, w, dims, preferred_element_type=F32)
    return both[:ROWS] + both[ROWS:]


def stack(v):
    return jnp.concatenate(split(v), axis=0)


def outer3(a, b):
    ah, al = split(a)
    bh, bl = split(b)
    return lax.dot_general(
        jnp.concatenate([ah, ah, al], axis=0),
        jnp.concatenate([bh, bl, bh], axis=0),
        TN,
        preferred_element_type=F32,
    )


def mean(v):
    return jnp.mean(v, axis=-1, keepdims=True)


def norm(v):
    c = v - mean(v)
    r = lax.rsqrt(mean(c * c) + 1e-05)
    return c * r, r


def norm_back(dy, y, r):
    return r * (dy - mean(dy) - y * mean(dy * y))


def place(ref, v):
    for h in range(2):
        for r in range(2):
            ref[2 * h + r] = v[r * PART : (r + 1) * PART, h * 128 : (h + 1) * 128]


def whole(ref):
    return jnp.concatenate(
        [jnp.concatenate([ref[2 * h], ref[2 * h + 1]], axis=0) for h in range(2)], axis=1
    )


class Place:
    def __init__(self):
        dp, tile = lax.axis_index("dp"), lax.axis_index("tile")
        self.tile = tile
        self.c = lax.rem(dp, 2)
        self.x = lax.rem(dp // 2, X)
        self.zl = dp // (2 * X)
        self.y = lax.rem(tile, Y)
        self.zh = tile // Y

    def at(self, dx=0, dy=0, dzl=0, dzh=0, dc=0):
        x = lax.rem(self.x + dx, X)
        y = lax.rem(self.y + dy, Y)
        zl = lax.rem(self.zl + dzl, ZL)
        zh = lax.rem(self.zh + dzh, ZH)
        c = lax.rem(self.c + dc, 2)
        return ((zl * X + x) * 2 + c, zh * Y + y)


class Sems:
    def __init__(self, send, recv):
        self.send, self.recv, self.n = send, recv, 0

    def copy(self, src, dst, device):
        i = self.n
        self.n += 1
        return pltpu.make_async_remote_copy(
            src_ref=src,
            dst_ref=dst,
            send_sem=self.send.at[i],
            recv_sem=self.recv.at[i],
            device_id=device,
            device_id_type=MESH,
        )


class TileSum:
    def __init__(self, me, sems, mine, got, pair, total):
        self.me, self.sems = me, sems
        self.mine, self.got, self.pair, self.total = mine, got, pair, total
        self.all = []

    def start(self, copies):
        for c in copies:
            c.start()
        self.all += copies
        return copies

    def scatter(self):
        me = self.me
        self.a = self.start(
            [
                self.sems.copy(self.mine.at[lax.rem(me.y + d, Y)], self.got.at[d - 1], me.at(dy=d))
                for d in (1, 2, 3)
            ]
        )

    def exchange(self):
        for c in self.a:
            c.wait_recv()
        me = self.me
        self.pair[0] = (self.mine[me.y] + self.got[0]) + (self.got[1] + self.got[2])
        self.b = self.start([self.sems.copy(self.pair.at[0], self.pair.at[1], me.at(dzh=1))])

    def gather(self):
        self.b[0].wait_recv()
        me = self.me
        self.total[me.y] = self.pair[0] + self.pair[1]
        here = self.total.at[me.y]
        self.d = self.start([self.sems.copy(here, here, me.at(dy=d)) for d in (1, 2, 3)])

    def result(self):
        for c in self.d:
            c.wait_recv()
        return whole(self.total)

    def close(self):
        for c in self.all:
            c.wait_send()


def section(
    scale,
    feat_in,
    kern_in,
    cot_in,
    wfg_in,
    wval_in,
    wup_in,
    wdown_in,
    gathered,
    gf_out,
    gk_out,
    feat,
    cot,
    kern_v,
    prob,
    prob_b,
    dlog,
    wfg,
    wval,
    wup,
    wdown,
    acc,
    acc2,
    hid,
    slope,
    dhid,
    tmp,
    sums,
    got,
    pair,
    total,
    terms,
    r0,
    mine,
    r1,
    half,
    r2,
    small,
    local,
    send,
    recv,
):
    me = Place()
    sems = Sems(send, recv)
    n = kern_in.shape[0]
    cells = feat_in.shape[0]
    chunks = cells // CHUNK
    ff = wup_in.shape[1] // 256
    c, x, y, zl, zh = me.c, me.x, me.y, me.zl, me.zh

    def part(i):
        return pl.ds(pl.multiple_of(i * CHUNK, CHUNK), CHUNK)

    def feat_copy(i):
        return pltpu.make_async_copy(feat_in.at[part(i), :], feat.at[part(i), :], local.at[i])

    def cot_copy(i):
        return pltpu.make_async_copy(cot_in.at[:, part(i)], cot.at[:, part(i)], local.at[chunks + i])

    kern_copy = pltpu.make_async_copy(kern_in, kern_v, local.at[2 * chunks + 4])
    kern_copy.start()
    for i in range(chunks):
        feat_copy(i).start()
    for i in range(chunks):
        cot_copy(i).start()
    base = 2 * chunks
    weights = [
        pltpu.make_async_copy(a, b, local.at[base + i])
        for i, (a, b) in enumerate(((wfg_in, wfg), (wval_in, wval), (wup_in, wup), (wdown_in, wdown)))
    ]
    for w in weights:
        w.start()

    partners = [me.at(dc=1)]
    partners += [me.at(dy=d) for d in (1, 2, 3)]
    partners += [me.at(dx=d) for d in (1, 2, 3)]
    partners += [me.at(dzl=d % ZL, dzh=d // ZL) for d in range(1, ZL * ZH)]
    barrier = pltpu.get_barrier_semaphore()
    for p in partners:
        pl.semaphore_signal(barrier, inc=1, device_id=p, device_id_type=MESH)

    kern_copy.wait()
    kern = kern_v[...]

    acc[...] = jnp.zeros_like(acc)

    def pool(i, carry):
        feat_copy(i).wait()
        f = feat[part(i), :]
        p = jax.nn.sigmoid(lax.dot_general(kern, f, NT, preferred_element_type=F32))
        prob[:, part(i)] = p
        pb = p.astype(BF16)
        prob_b[:, part(i)] = pb
        acc[:n, :] += jnp.dot(pb, f, preferred_element_type=F32)
        return carry

    lax.fori_loop(0, chunks, pool, 0)
    sum_p = TileSum(me, sems, sums.at[0], got.at[0], pair.at[0], total.at[0])
    sum_d = TileSum(me, sems, sums.at[1], got.at[1], pair.at[1], total.at[1])
    sum_m = TileSum(me, sems, sums.at[2], got.at[2], pair.at[2], total.at[2])
    place(sums.at[0], acc[...])
    pl.semaphore_wait(barrier, len(partners))
    sum_p.scatter()

    acc[...] = jnp.zeros_like(acc)

    def new(i, carry):
        cot_copy(i).wait()
        acc[:n, :] += jnp.dot(cot[:, part(i)], feat[part(i), :], preferred_element_type=F32)
        return carry

    lax.fori_loop(0, chunks, new, 0)
    place(sums.at[1], acc[...])
    sum_d.scatter()
    sum_p.exchange()
    sum_d.exchange()
    for w in weights:
        w.wait()
    acc[...] = jnp.zeros_like(acc)
    acc[:n, :] = kern.astype(F32)
    kern32 = acc[...]
    sum_p.gather()
    sum_d.gather()

    pooled = sum_p.result() * scale
    pooled2 = stack(pooled)
    gate = jax.nn.sigmoid(dot2(pooled2, wfg[...], NN))
    value = dot2(pooled2, wval[...], NN)
    k1, rs1 = norm(gate * value + kern32)
    k1s = stack(k1)
    z = k1
    for j in range(ff):
        a = dot2(k1s, wup[:, j * 256 : (j + 1) * 256], NN)
        t = jnp.tanh(0.7978845608028654 * (a + 0.044715 * (a * a * a)))
        up = 0.5 * (1.0 + t)
        h = a * up
        hid[j] = h
        slope[j] = up + 0.5 * a * (1.0 - t * t) * (0.7978845608028654 * (1.0 + 0.134145 * (a * a)))
        z = z + dot2(stack(h), wdown[j * 256 : (j + 1) * 256, :], NN)
    k3, rs3 = norm(z)
    newk = k3.astype(BF16)[:n]

    dz = norm_back(sum_d.result(), k3, rs3)
    dzs = stack(dz)
    dk1 = dz
    for j in range(ff):
        da = dot2(dzs, wdown[j * 256 : (j + 1) * 256, :], NT) * slope[j]
        dhid[j] = da
        dk1 = dk1 + dot2(stack(da), wup[:, j * 256 : (j + 1) * 256], NT)
    du = norm_back(dk1, k1, rs1)
    dgate = du * value * (gate * (1.0 - gate))
    dvalue = du * gate
    dpooled = dot2(stack(dgate), wfg[...], NT) + dot2(stack(dvalue), wval[...], NT)
    dscaled = (dpooled * scale).astype(BF16)
    acc[...] = du

    up_term = outer3(k1, dhid[me.tile])
    down_term = outer3(hid[me.tile], dz)
    tmp[0] = outer3(pooled, dgate)
    tmp[1] = outer3(pooled, dvalue)
    for h in range(2):
        lanes = slice(h * 128, (h + 1) * 128)
        for i in range(X):
            own = pl.ds(pl.multiple_of(me.tile * 32 + i * 8, 8), 8)
            terms[h, i, :64, :] = up_term[i * 64 : (i + 1) * 64, lanes]
            terms[h, i, 64:128, :] = down_term[i * 64 : (i + 1) * 64, lanes]
            terms[h, i, 128:136, :] = tmp[0, own, lanes]
            terms[h, i, 136:, :] = tmp[1, own, lanes]
    c0 = sems.copy(terms.at[1 - c], r0, me.at(dc=1))
    c0.start()

    ds = dscaled[:n]

    def mask(i, carry):
        f = feat[part(i), :]
        p = prob[:, part(i)]
        dp = lax.dot_general(ds, f, NT, preferred_element_type=F32)
        dl = (dp * p * (1.0 - p)).astype(BF16)
        dlog[:, part(i)] = dl
        return carry + jnp.dot(dl, f, preferred_element_type=F32)

    def term(a, b):
        return lax.dot_general(a, b, TN, preferred_element_type=F32)

    def features(i):
        gf_out[part(i), :] = (
            term(cot[:, part(i)], newk) + term(prob_b[:, part(i)], ds) + term(dlog[:, part(i)], kern)
        )

    macc = lax.fori_loop(0, 2, mask, jnp.zeros((n, 256), F32))
    c0.wait_recv()
    mine[...] = terms[c] + r0[...]
    c1 = [sems.copy(mine.at[lax.rem(x + d, X)], r1.at[d - 1], me.at(dx=d)) for d in (1, 3, 2)]
    for cp in c1:
        cp.start()
    macc = lax.fori_loop(2, chunks, mask, macc)
    acc2[...] = jnp.zeros_like(acc2)
    acc2[:n, :] = macc
    place(sums.at[2], acc2[...])
    sum_m.scatter()
    for cp in c1:
        cp.wait_recv()
    half[...] = (mine[x] + r1[0]) + (r1[1] + r1[2])

    def piece(i):
        return pl.ds(pl.multiple_of(i * PIECE, PIECE), PIECE)

    tail = pl.ds(ZL * PIECE, SMALL)
    small[zl] = half[ZL * PIECE :, :]
    c2 = []
    for d in (1, 3, 2):
        c2.append(sems.copy(half.at[piece(lax.rem(zl + d, ZL)), :], r2.at[d - 1], me.at(dzl=d)))
        c2.append(sems.copy(half.at[tail, :], small.at[zl], me.at(dzl=d)))
    for cp in c2:
        cp.start()
    sum_m.exchange()
    features(0)
    for cp in c2:
        cp.wait_recv()

    gathered[c, zh, y, x, piece(zl), :] = (half[piece(zl), :] + r2[0]) + (r2[1] + r2[2])
    gathered[c, zh, y, x, tail, :] = (small[0] + small[1]) + (small[2] + small[3])
    here = gathered.at[c, zh, y, x, piece(zl), :]
    here_tail = gathered.at[c, zh, y, x, tail, :]
    far = [sems.copy(here, here, me.at(dzl=d, dzh=1)) for d in (0, 1, 3, 2)]
    far.append(sems.copy(here_tail, here_tail, me.at(dzh=1)))
    near = [sems.copy(here, here, me.at(dzl=d)) for d in (1, 3, 2)]
    for cp in near + far:
        cp.start()
    sum_m.gather()
    features(1)

    mx, my = 1 - c, c

    def block(q, m, l):
        bx = lax.rem(x + mx * m + my * l, X)
        by = lax.rem(y + my * m + mx * l, Y)
        return gathered.at[c, lax.rem(zh + q, ZH), by, bx]

    started = []
    twin = []

    def send_to(b, device):
        cp = sems.copy(b, b, device)
        cp.start()
        started.append(cp)
        return cp

    def along_mid(d):
        return me.at(dx=mx * d, dy=my * d)

    def along_last(d):
        return me.at(dx=my * d, dy=mx * d)

    def to_twin(b):
        twin.append(send_to(b, me.at(dc=1)))

    mids, lasts, halves = {}, {}, {}

    def open_mid(q):
        b = block(q, 0, 0)
        for d in (1, 3, 2):
            mids[q, d] = send_to(b, along_mid(d))

    def open_last(q, m):
        if m:
            mids[q, m].wait_recv()
        b = block(q, (4 - m) % 4, 0)
        lasts[q, m] = [send_to(b, along_last(d)) for d in (1, 3)]
        to_twin(b)

    def relay(q, m):
        halves[q, m] = []
        for d, first, cp in zip((1, 3), (0, BLOCK // 2), lasts[q, m]):
            cp.wait_recv()
            b = block(q, (4 - m) % 4, 4 - d)
            halves[q, m].append(send_to(b.at[pl.ds(first, BLOCK // 2), :], along_last(d)))
            to_twin(b)

    def close(q, m):
        for cp in halves[q, m]:
            cp.wait_recv()
        to_twin(block(q, (4 - m) % 4, 2))

    for cp in near:
        cp.wait_recv()
    open_mid(0)
    open_last(0, 0)
    features(2)
    for cp in far:
        cp.wait_recv()
    open_mid(1)
    open_last(1, 0)
    features(3)
    relay(0, 0)
    open_last(0, 1)
    open_last(0, 3)
    relay(1, 0)
    open_last(1, 1)
    open_last(1, 3)
    open_last(0, 2)
    open_last(1, 2)
    close(0, 0)
    features(4)
    relay(0, 1)
    relay(0, 3)
    close(1, 0)
    relay(1, 1)
    relay(1, 3)
    gk_out[:, 0, :] = (sum_m.result() + acc[...])[:n]
    close(0, 1)
    close(0, 3)
    relay(0, 2)
    relay(1, 2)
    close(1, 1)
    close(1, 3)
    close(0, 2)
    close(1, 2)
    for cp in twin:
        cp.wait_recv()

    for s in (sum_p, sum_d, sum_m):
        s.close()
    for cp in [c0] + c1 + c2 + near + far + started:
        cp.wait_send()


def finish(gathered, gf, gk, grad_f, grad_k, g_gate, g_value, g_up, g_down, sem):
    pairs = [(gf, grad_f), (gk, grad_k)]
    for h in range(2):
        lanes = pl.ds(h * 128, 128)
        for t in range(ZH * Y):
            src = gathered.at[h, t // Y, t % Y]
            pairs += [
                (src.at[:, 0:64, :], g_up.at[:, :, pl.ds(t * 256 + h * 128, 128)]),
                (src.at[:, 64:128, :], g_down.at[t, :, :, lanes]),
                (src.at[:, 128:136, :], g_gate.at[t, :, :, lanes]),
                (src.at[:, 136:144, :], g_value.at[t, :, :, lanes]),
            ]
    copies = [pltpu.make_async_copy(a, b, sem.at[i]) for i, (a, b) in enumerate(pairs)]
    for cp in copies:
        cp.start()
    for cp in copies:
        cp.wait()


def shards(features, kernels, cotangent, w_feat_gate, w_value, w_up, w_down):
    feat, kern, cot = features[0], kernels[0], cotangent[0]
    n, channels = kern.shape
    cells = feat.shape[0]
    chunks = cells // CHUNK
    ff = w_up.shape[1] // 256
    scale = 1.0 / math.sqrt(lax.axis_size("tile") * cells)
    anywhere = pl.BlockSpec(memory_space=pl.ANY)

    def hbm(v):
        return pltpu.with_memory_space_constraint(v, pltpu.HBM)

    kern, cot = hbm(kern), hbm(cot)
    vmem = pl.BlockSpec(memory_space=pltpu.VMEM)
    copies = 128
    shape = jax.ShapeDtypeStruct
    gathered, gf, gk = pl.pallas_call(
        functools.partial(section, scale),
        out_shape=(
            shape((2, ZH, Y, X, BLOCK, 128), F32),
            shape((cells, channels), F32),
            shape((n, 1, channels), F32),
        ),
        in_specs=[anywhere] * 7,
        out_specs=(vmem, vmem, vmem),
        scratch_shapes=[
            pltpu.VMEM((cells, channels), BF16),
            pltpu.VMEM((n, cells), BF16),
            pltpu.VMEM((n, channels), BF16),
            pltpu.VMEM((n, cells), F32),
            pltpu.VMEM((n, cells), BF16),
            pltpu.VMEM((n, cells), BF16),
            pltpu.VMEM(w_feat_gate.shape, BF16),
            pltpu.VMEM(w_value.shape, BF16),
            pltpu.VMEM(w_up.shape, BF16),
            pltpu.VMEM(w_down.shape, BF16),
            pltpu.VMEM((ROWS, channels), F32),
            pltpu.VMEM((ROWS, channels), F32),
            pltpu.VMEM((ff, ROWS, 256), F32),
            pltpu.VMEM((ff, ROWS, 256), F32),
            pltpu.VMEM((ff, ROWS, 256), F32),
            pltpu.VMEM((2, 256, 256), F32),
            pltpu.VMEM((3, 4, PART, 128), F32),
            pltpu.VMEM((3, 3, PART, 128), F32),
            pltpu.VMEM((3, 2, PART, 128), F32),
            pltpu.VMEM((3, 4, PART, 128), F32),
            pltpu.VMEM((2, X, BLOCK, 128), F32),
            pltpu.VMEM((X, BLOCK, 128), F32),
            pltpu.VMEM((X, BLOCK, 128), F32),
            pltpu.VMEM((3, BLOCK, 128), F32),
            pltpu.VMEM((BLOCK, 128), F32),
            pltpu.VMEM((3, PIECE, 128), F32),
            pltpu.VMEM((ZL, SMALL, 128), F32),
            pltpu.SemaphoreType.DMA((2 * chunks + 5,)),
            pltpu.SemaphoreType.DMA((copies,)),
            pltpu.SemaphoreType.DMA((copies,)),
        ],
        compiler_params=pltpu.CompilerParams(
            collective_id=0, has_side_effects=True, vmem_limit_bytes=32 * 2**20
        ),
        name="section",
    )(hbm(feat), kern, cot, hbm(w_feat_gate), hbm(w_value), hbm(w_up), hbm(w_down))

    tiles = ZH * Y
    grad_f, grad_k, g_gate, g_value, g_up, g_down = pl.pallas_call(
        finish,
        out_shape=(
            shape((cells, channels), F32),
            shape((n, 1, channels), F32),
            shape((tiles, X, 8, channels), F32),
            shape((tiles, X, 8, channels), F32),
            shape((X, 64, w_up.shape[1]), F32),
            shape((tiles, X, 64, channels), F32),
        ),
        in_specs=[anywhere] * 3,
        out_specs=(anywhere,) * 6,
        scratch_shapes=[pltpu.SemaphoreType.DMA((2 + tiles * 2 * 4,))],
        name="finish",
    )(gathered, gf, gk)
    return (
        grad_f[None],
        jnp.transpose(grad_k, (1, 0, 2)),
        g_gate.reshape(w_feat_gate.shape),
        g_value.reshape(w_value.shape),
        g_up.reshape(w_up.shape),
        g_down.reshape(w_down.shape),
    )


def solution(mesh):
    placed = (P("dp", "tile", None), P("dp", None, None), P("dp", None, "tile"), P(), P(), P(), P())
    return jax.shard_map(
        shards,
        mesh=mesh,
        in_specs=placed,
        out_specs=(P("dp", "tile", None), P("dp", None, None), P(), P(), P(), P()),
        check_vma=False,
    )
```

```python
import functools
import math

import jax
import jax.numpy as jnp
from jax import lax
from jax.experimental import pallas as pl
from jax.experimental.pallas import tpu as pltpu
from jax.sharding import PartitionSpec as P

MESH = pl.DeviceIdType.MESH
F32, BF16 = jnp.float32, jnp.bfloat16
X, Y, ZL, ZH = 4, 4, 4, 2
ROWS = 112
PART = 56
CHUNK = 1024
PIECE = 32
SMALL = 16
BLOCK = ZL * PIECE + SMALL
NT = (((1,), (1,)), ((), ()))
NN = (((1,), (0,)), ((), ()))
TN = (((0,), (0,)), ((), ()))


def split(v):
    hi = v.astype(BF16)
    return hi, (v - hi.astype(F32)).astype(BF16)


def dot2(stacked, w, dims):
    both = lax.dot_general(stacked, w, dims, preferred_element_type=F32)
    return both[:ROWS] + both[ROWS:]


def stack(v):
    return jnp.concatenate(split(v), axis=0)


def outer3(a, b):
    ah, al = split(a)
    bh, bl = split(b)
    return lax.dot_general(
        jnp.concatenate([ah, ah, al], axis=0),
        jnp.concatenate([bh, bl, bh], axis=0),
        TN,
        preferred_element_type=F32,
    )


def mean(v):
    return jnp.mean(v, axis=-1, keepdims=True)


def norm(v):
    c = v - mean(v)
    r = lax.rsqrt(mean(c * c) + 1e-05)
    return c * r, r


def norm_back(dy, y, r):
    return r * (dy - mean(dy) - y * mean(dy * y))


def place(ref, v):
    for h in range(2):
        for r in range(2):
            ref[2 * h + r] = v[r * PART : (r + 1) * PART, h * 128 : (h + 1) * 128]


def whole(ref):
    return jnp.concatenate(
        [jnp.concatenate([ref[2 * h], ref[2 * h + 1]], axis=0) for h in range(2)], axis=1
    )


class Place:
    def __init__(self):
        dp, tile = lax.axis_index("dp"), lax.axis_index("tile")
        self.tile = tile
        self.c = lax.rem(dp, 2)
        self.x = lax.rem(dp // 2, X)
        self.zl = dp // (2 * X)
        self.y = lax.rem(tile, Y)
        self.zh = tile // Y

    def at(self, dx=0, dy=0, dzl=0, dzh=0, dc=0):
        x = lax.rem(self.x + dx, X)
        y = lax.rem(self.y + dy, Y)
        zl = lax.rem(self.zl + dzl, ZL)
        zh = lax.rem(self.zh + dzh, ZH)
        c = lax.rem(self.c + dc, 2)
        return ((zl * X + x) * 2 + c, zh * Y + y)


class Sems:
    def __init__(self, send, recv):
        self.send, self.recv, self.n = send, recv, 0

    def copy(self, src, dst, device):
        i = self.n
        self.n += 1
        return pltpu.make_async_remote_copy(
            src_ref=src,
            dst_ref=dst,
            send_sem=self.send.at[i],
            recv_sem=self.recv.at[i],
            device_id=device,
            device_id_type=MESH,
        )


class TileSum:
    def __init__(self, me, sems, mine, got, pair, total):
        self.me, self.sems = me, sems
        self.mine, self.got, self.pair, self.total = mine, got, pair, total
        self.all = []

    def start(self, copies):
        for c in copies:
            c.start()
        self.all += copies
        return copies

    def scatter(self):
        me = self.me
        self.a = self.start(
            [
                self.sems.copy(self.mine.at[lax.rem(me.y + d, Y)], self.got.at[d - 1], me.at(dy=d))
                for d in (1, 2, 3)
            ]
        )

    def exchange(self):
        for c in self.a:
            c.wait_recv()
        me = self.me
        self.pair[0] = (self.mine[me.y] + self.got[0]) + (self.got[1] + self.got[2])
        self.b = self.start([self.sems.copy(self.pair.at[0], self.pair.at[1], me.at(dzh=1))])

    def gather(self):
        self.b[0].wait_recv()
        me = self.me
        self.total[me.y] = self.pair[0] + self.pair[1]
        here = self.total.at[me.y]
        self.d = self.start([self.sems.copy(here, here, me.at(dy=d)) for d in (1, 2, 3)])

    def result(self):
        for c in self.d:
            c.wait_recv()
        return whole(self.total)

    def close(self):
        for c in self.all:
            c.wait_send()


def section(
    scale,
    feat_in,
    kern_in,
    cot_in,
    wfg_in,
    wval_in,
    wup_in,
    wdown_in,
    gathered,
    gf_out,
    gk_out,
    feat,
    cot,
    kern_v,
    prob,
    prob_b,
    dlog,
    wfg,
    wval,
    wup,
    wdown,
    acc,
    acc2,
    hid,
    slope,
    dhid,
    tmp,
    sums,
    got,
    pair,
    total,
    terms,
    r0,
    mine,
    r1,
    half,
    r2,
    small,
    local,
    send,
    recv,
):
    me = Place()
    sems = Sems(send, recv)
    n = kern_in.shape[0]
    cells = feat_in.shape[0]
    chunks = cells // CHUNK
    ff = wup_in.shape[1] // 256
    c, x, y, zl, zh = me.c, me.x, me.y, me.zl, me.zh

    def part(i):
        return pl.ds(pl.multiple_of(i * CHUNK, CHUNK), CHUNK)

    def feat_copy(i):
        return pltpu.make_async_copy(feat_in.at[part(i), :], feat.at[part(i), :], local.at[i])

    def cot_copy(i):
        return pltpu.make_async_copy(cot_in.at[:, part(i)], cot.at[:, part(i)], local.at[chunks + i])

    kern_copy = pltpu.make_async_copy(kern_in, kern_v, local.at[2 * chunks + 4])
    kern_copy.start()
    for i in range(chunks):
        feat_copy(i).start()
    for i in range(chunks):
        cot_copy(i).start()
    base = 2 * chunks
    weights = [
        pltpu.make_async_copy(a, b, local.at[base + i])
        for i, (a, b) in enumerate(((wfg_in, wfg), (wval_in, wval), (wup_in, wup), (wdown_in, wdown)))
    ]
    for w in weights:
        w.start()

    partners = [me.at(dc=1)]
    partners += [me.at(dy=d) for d in (1, 2, 3)]
    partners += [me.at(dx=d) for d in (1, 2, 3)]
    partners += [me.at(dzl=d % ZL, dzh=d // ZL) for d in range(1, ZL * ZH)]
    barrier = pltpu.get_barrier_semaphore()
    for p in partners:
        pl.semaphore_signal(barrier, inc=1, device_id=p, device_id_type=MESH)

    kern_copy.wait()
    kern = kern_v[...]

    acc[...] = jnp.zeros_like(acc)

    def pool(i, carry):
        feat_copy(i).wait()
        f = feat[part(i), :]
        p = jax.nn.sigmoid(lax.dot_general(kern, f, NT, preferred_element_type=F32))
        prob[:, part(i)] = p
        pb = p.astype(BF16)
        prob_b[:, part(i)] = pb
        acc[:n, :] += jnp.dot(pb, f, preferred_element_type=F32)
        return carry

    lax.fori_loop(0, chunks, pool, 0)
    sum_p = TileSum(me, sems, sums.at[0], got.at[0], pair.at[0], total.at[0])
    sum_d = TileSum(me, sems, sums.at[1], got.at[1], pair.at[1], total.at[1])
    sum_m = TileSum(me, sems, sums.at[2], got.at[2], pair.at[2], total.at[2])
    place(sums.at[0], acc[...])
    pl.semaphore_wait(barrier, len(partners))
    sum_p.scatter()

    acc[...] = jnp.zeros_like(acc)

    def new(i, carry):
        cot_copy(i).wait()
        acc[:n, :] += jnp.dot(cot[:, part(i)], feat[part(i), :], preferred_element_type=F32)
        return carry

    lax.fori_loop(0, chunks, new, 0)
    place(sums.at[1], acc[...])
    sum_d.scatter()
    sum_p.exchange()
    sum_d.exchange()
    for w in weights:
        w.wait()
    acc[...] = jnp.zeros_like(acc)
    acc[:n, :] = kern.astype(F32)
    kern32 = acc[...]
    sum_p.gather()
    sum_d.gather()

    pooled = sum_p.result() * scale
    pooled2 = stack(pooled)
    gate = jax.nn.sigmoid(dot2(pooled2, wfg[...], NN))
    value = dot2(pooled2, wval[...], NN)
    k1, rs1 = norm(gate * value + kern32)
    k1s = stack(k1)
    z = k1
    for j in range(ff):
        a = dot2(k1s, wup[:, j * 256 : (j + 1) * 256], NN)
        t = jnp.tanh(0.7978845608028654 * (a + 0.044715 * (a * a * a)))
        up = 0.5 * (1.0 + t)
        h = a * up
        hid[j] = h
        slope[j] = up + 0.5 * a * (1.0 - t * t) * (0.7978845608028654 * (1.0 + 0.134145 * (a * a)))
        z = z + dot2(stack(h), wdown[j * 256 : (j + 1) * 256, :], NN)
    k3, rs3 = norm(z)
    newk = k3.astype(BF16)[:n]

    dz = norm_back(sum_d.result(), k3, rs3)
    dzs = stack(dz)
    dk1 = dz
    for j in range(ff):
        da = dot2(dzs, wdown[j * 256 : (j + 1) * 256, :], NT) * slope[j]
        dhid[j] = da
        dk1 = dk1 + dot2(stack(da), wup[:, j * 256 : (j + 1) * 256], NT)
    du = norm_back(dk1, k1, rs1)
    dgate = du * value * (gate * (1.0 - gate))
    dvalue = du * gate
    dpooled = dot2(stack(dgate), wfg[...], NT) + dot2(stack(dvalue), wval[...], NT)
    dscaled = (dpooled * scale).astype(BF16)
    acc[...] = du

    up_term = outer3(k1, dhid[me.tile])
    down_term = outer3(hid[me.tile], dz)
    tmp[0] = outer3(pooled, dgate)
    tmp[1] = outer3(pooled, dvalue)
    for h in range(2):
        lanes = slice(h * 128, (h + 1) * 128)
        for i in range(X):
            own = pl.ds(pl.multiple_of(me.tile * 32 + i * 8, 8), 8)
            terms[h, i, :64, :] = up_term[i * 64 : (i + 1) * 64, lanes]
            terms[h, i, 64:128, :] = down_term[i * 64 : (i + 1) * 64, lanes]
            terms[h, i, 128:136, :] = tmp[0, own, lanes]
            terms[h, i, 136:, :] = tmp[1, own, lanes]
    c0 = sems.copy(terms.at[1 - c], r0, me.at(dc=1))
    c0.start()

    ds = dscaled[:n]

    def mask(i, carry):
        f = feat[part(i), :]
        p = prob[:, part(i)]
        dp = lax.dot_general(ds, f, NT, preferred_element_type=F32)
        dl = (dp * p * (1.0 - p)).astype(BF16)
        dlog[:, part(i)] = dl
        return carry + jnp.dot(dl, f, preferred_element_type=F32)

    def term(a, b):
        return lax.dot_general(a, b, TN, preferred_element_type=F32)

    def features(i):
        gf_out[part(i), :] = (
            term(cot[:, part(i)], newk) + term(prob_b[:, part(i)], ds) + term(dlog[:, part(i)], kern)
        )

    macc = lax.fori_loop(0, 2, mask, jnp.zeros((n, 256), F32))
    c0.wait_recv()
    mine[...] = terms[c] + r0[...]
    c1 = [sems.copy(mine.at[lax.rem(x + d, X)], r1.at[d - 1], me.at(dx=d)) for d in (1, 3, 2)]
    for cp in c1:
        cp.start()
    macc = lax.fori_loop(2, chunks, mask, macc)
    acc2[...] = jnp.zeros_like(acc2)
    acc2[:n, :] = macc
    place(sums.at[2], acc2[...])
    sum_m.scatter()
    for cp in c1:
        cp.wait_recv()
    half[...] = (mine[x] + r1[0]) + (r1[1] + r1[2])

    def piece(i):
        return pl.ds(pl.multiple_of(i * PIECE, PIECE), PIECE)

    tail = pl.ds(ZL * PIECE, SMALL)
    small[zl] = half[ZL * PIECE :, :]
    c2 = []
    for d in (1, 3, 2):
        c2.append(sems.copy(half.at[piece(lax.rem(zl + d, ZL)), :], r2.at[d - 1], me.at(dzl=d)))
        c2.append(sems.copy(half.at[tail, :], small.at[zl], me.at(dzl=d)))
    for cp in c2:
        cp.start()
    sum_m.exchange()
    features(0)
    for cp in c2:
        cp.wait_recv()

    gathered[c, zh, y, x, piece(zl), :] = (half[piece(zl), :] + r2[0]) + (r2[1] + r2[2])
    gathered[c, zh, y, x, tail, :] = (small[0] + small[1]) + (small[2] + small[3])
    here = gathered.at[c, zh, y, x, piece(zl), :]
    here_tail = gathered.at[c, zh, y, x, tail, :]
    far = [sems.copy(here, here, me.at(dzl=d, dzh=1)) for d in (0, 1, 3, 2)]
    far.append(sems.copy(here_tail, here_tail, me.at(dzh=1)))
    near = [sems.copy(here, here, me.at(dzl=d)) for d in (1, 3, 2)]
    for cp in near + far:
        cp.start()
    sum_m.gather()
    features(1)

    mx, my = 1 - c, c

    def block(q, m, l):
        bx = lax.rem(x + mx * m + my * l, X)
        by = lax.rem(y + my * m + mx * l, Y)
        return gathered.at[c, lax.rem(zh + q, ZH), by, bx]

    started = []
    twin = []

    def send_to(b, device):
        cp = sems.copy(b, b, device)
        cp.start()
        started.append(cp)
        return cp

    def along_mid(d):
        return me.at(dx=mx * d, dy=my * d)

    def along_last(d):
        return me.at(dx=my * d, dy=mx * d)

    def to_twin(b):
        twin.append(send_to(b, me.at(dc=1)))

    mids, lasts, halves = {}, {}, {}

    def open_mid(q):
        b = block(q, 0, 0)
        for d in (1, 3, 2):
            mids[q, d] = send_to(b, along_mid(d))

    def open_last(q, m):
        if m:
            mids[q, m].wait_recv()
        b = block(q, (4 - m) % 4, 0)
        lasts[q, m] = [send_to(b, along_last(d)) for d in (1, 3)]
        to_twin(b)

    def relay(q, m):
        halves[q, m] = []
        for d, first, cp in zip((1, 3), (0, BLOCK // 2), lasts[q, m]):
            cp.wait_recv()
            b = block(q, (4 - m) % 4, 4 - d)
            halves[q, m].append(send_to(b.at[pl.ds(first, BLOCK // 2), :], along_last(d)))
            to_twin(b)

    def close(q, m):
        for cp in halves[q, m]:
            cp.wait_recv()
        to_twin(block(q, (4 - m) % 4, 2))

    for cp in near:
        cp.wait_recv()
    open_mid(0)
    open_last(0, 0)
    features(2)
    for cp in far:
        cp.wait_recv()
    open_mid(1)
    open_last(1, 0)
    features(3)
    relay(0, 0)
    open_last(0, 1)
    open_last(0, 3)
    relay(1, 0)
    open_last(1, 1)
    open_last(1, 3)
    open_last(0, 2)
    open_last(1, 2)
    close(0, 0)
    features(4)
    relay(0, 1)
    relay(0, 3)
    close(1, 0)
    relay(1, 1)
    relay(1, 3)
    gk_out[:, 0, :] = (sum_m.result() + acc[...])[:n]
    close(0, 1)
    close(0, 3)
    relay(0, 2)
    relay(1, 2)
    close(1, 1)
    close(1, 3)
    close(0, 2)
    close(1, 2)
    for cp in twin:
        cp.wait_recv()

    for s in (sum_p, sum_d, sum_m):
        s.close()
    for cp in [c0] + c1 + c2 + near + far + started:
        cp.wait_send()


def finish(gathered, gf, gk, grad_f, grad_k, g_gate, g_value, g_up, g_down, sem):
    pairs = [(gf, grad_f), (gk, grad_k)]
    for h in range(2):
        lanes = pl.ds(h * 128, 128)
        for t in range(ZH * Y):
            src = gathered.at[h, t // Y, t % Y]
            pairs += [
                (src.at[:, 0:64, :], g_up.at[:, :, pl.ds(t * 256 + h * 128, 128)]),
                (src.at[:, 64:128, :], g_down.at[t, :, :, lanes]),
                (src.at[:, 128:136, :], g_gate.at[t, :, :, lanes]),
                (src.at[:, 136:144, :], g_value.at[t, :, :, lanes]),
            ]
    copies = [pltpu.make_async_copy(a, b, sem.at[i]) for i, (a, b) in enumerate(pairs)]
    for cp in copies:
        cp.start()
    for cp in copies:
        cp.wait()


def shards(features, kernels, cotangent, w_feat_gate, w_value, w_up, w_down):
    feat, kern, cot = features[0], kernels[0], cotangent[0]
    n, channels = kern.shape
    cells = feat.shape[0]
    chunks = cells // CHUNK
    ff = w_up.shape[1] // 256
    scale = 1.0 / math.sqrt(lax.axis_size("tile") * cells)
    anywhere = pl.BlockSpec(memory_space=pl.ANY)

    def hbm(v):
        return pltpu.with_memory_space_constraint(v, pltpu.HBM)

    def vmem_array(v):
        return pltpu.with_memory_space_constraint(v, pltpu.VMEM)

    vmem = pl.BlockSpec(memory_space=pltpu.VMEM)
    copies = 128
    shape = jax.ShapeDtypeStruct
    gathered, gf, gk = pl.pallas_call(
        functools.partial(section, scale),
        out_shape=(
            shape((2, ZH, Y, X, BLOCK, 128), F32),
            shape((cells, channels), F32),
            shape((n, 1, channels), F32),
        ),
        in_specs=[anywhere] * 7,
        out_specs=(vmem, vmem, vmem),
        scratch_shapes=[
            pltpu.VMEM((cells, channels), BF16),
            pltpu.VMEM((n, cells), BF16),
            pltpu.VMEM((n, channels), BF16),
            pltpu.VMEM((n, cells), F32),
            pltpu.VMEM((n, cells), BF16),
            pltpu.VMEM((n, cells), BF16),
            pltpu.VMEM(w_feat_gate.shape, BF16),
            pltpu.VMEM(w_value.shape, BF16),
            pltpu.VMEM(w_up.shape, BF16),
            pltpu.VMEM(w_down.shape, BF16),
            pltpu.VMEM((ROWS, channels), F32),
            pltpu.VMEM((ROWS, channels), F32),
            pltpu.VMEM((ff, ROWS, 256), F32),
            pltpu.VMEM((ff, ROWS, 256), F32),
            pltpu.VMEM((ff, ROWS, 256), F32),
            pltpu.VMEM((2, 256, 256), F32),
            pltpu.VMEM((3, 4, PART, 128), F32),
            pltpu.VMEM((3, 3, PART, 128), F32),
            pltpu.VMEM((3, 2, PART, 128), F32),
            pltpu.VMEM((3, 4, PART, 128), F32),
            pltpu.VMEM((2, X, BLOCK, 128), F32),
            pltpu.VMEM((X, BLOCK, 128), F32),
            pltpu.VMEM((X, BLOCK, 128), F32),
            pltpu.VMEM((3, BLOCK, 128), F32),
            pltpu.VMEM((BLOCK, 128), F32),
            pltpu.VMEM((3, PIECE, 128), F32),
            pltpu.VMEM((ZL, SMALL, 128), F32),
            pltpu.SemaphoreType.DMA((2 * chunks + 5,)),
            pltpu.SemaphoreType.DMA((copies,)),
            pltpu.SemaphoreType.DMA((copies,)),
        ],
        compiler_params=pltpu.CompilerParams(
            collective_id=0, has_side_effects=True, vmem_limit_bytes=32 * 2**20
        ),
        name="section",
    )(hbm(feat), hbm(kern), hbm(cot), hbm(w_feat_gate), hbm(w_value), hbm(w_up), hbm(w_down))

    tiles = ZH * Y
    grad_f, grad_k, g_gate, g_value, g_up, g_down = pl.pallas_call(
        finish,
        out_shape=(
            shape((cells, channels), F32),
            shape((n, 1, channels), F32),
            shape((tiles, X, 8, channels), F32),
            shape((tiles, X, 8, channels), F32),
            shape((X, 64, w_up.shape[1]), F32),
            shape((tiles, X, 64, channels), F32),
        ),
        in_specs=[vmem] * 3,
        out_specs=(anywhere,) * 6,
        scratch_shapes=[pltpu.SemaphoreType.DMA((2 + tiles * 2 * 4,))],
        compiler_params=pltpu.CompilerParams(vmem_limit_bytes=2**20),
        name="finish",
    )(vmem_array(gathered), vmem_array(gf), vmem_array(gk))
    return (
        grad_f[None],
        jnp.transpose(grad_k, (1, 0, 2)),
        g_gate.reshape(w_feat_gate.shape),
        g_value.reshape(w_value.shape),
        g_up.reshape(w_up.shape),
        g_down.reshape(w_down.shape),
    )


def solution(mesh):
    placed = (P("dp", "tile", None), P("dp", None, None), P("dp", None, "tile"), P(), P(), P(), P())
    return jax.shard_map(
        shards,
        mesh=mesh,
        in_specs=placed,
        out_specs=(P("dp", "tile", None), P("dp", None, None), P(), P(), P(), P()),
        check_vma=False,
    )
```

```python
import functools
import math

import jax
import jax.numpy as jnp
from jax import lax
from jax.experimental import pallas as pl
from jax.experimental.pallas import tpu as pltpu
from jax.sharding import PartitionSpec as P

MESH = pl.DeviceIdType.MESH
F32, BF16 = jnp.float32, jnp.bfloat16
X, Y, ZL, ZH = 4, 4, 4, 2
ROWS = 112
PART = 56
CHUNK = 1024
PIECE = 16
BLOCK = 144
PARTS = ((0, 64), (64, 80))
SMALL = (128, 16)
ORDER = [
    ("l", 0, 0, 1),
    ("l", 0, 0, 3),
    ("r", 0, 0, 0),
    ("l", 0, 0, 2),
    ("m", 1, 1, 0),
    ("l", 0, 1, 1),
    ("l", 0, 1, 3),
    ("r", 0, 1, 0),
    ("l", 1, 0, 1),
    ("l", 1, 0, 3),
    ("l", 0, 1, 2),
    ("r", 1, 0, 0),
    ("r", 0, 0, 1),
    ("l", 1, 0, 2),
    ("r", 1, 1, 0),
    ("r", 0, 0, 3),
    ("c", 0, 0, 0),
    ("r", 0, 1, 1),
    ("r", 0, 0, 2),
    ("r", 0, 1, 3),
    ("c", 0, 1, 0),
    ("l", 1, 1, 1),
    ("l", 1, 1, 3),
    ("r", 0, 1, 2),
    ("c", 1, 1, 0),
    ("c", 0, 1, 1),
    ("c", 0, 1, 3),
    ("l", 1, 1, 2),
    ("r", 1, 0, 1),
    ("r", 1, 0, 3),
    ("r", 1, 1, 1),
    ("c", 1, 0, 0),
    ("c", 0, 0, 1),
    ("r", 1, 1, 3),
    ("c", 0, 1, 2),
    ("r", 1, 0, 2),
    ("c", 0, 0, 3),
    ("r", 1, 1, 2),
    ("c", 0, 0, 2),
    ("c", 1, 1, 1),
    ("c", 1, 0, 1),
    ("c", 1, 0, 3),
    ("c", 1, 1, 3),
    ("c", 1, 0, 2),
    ("c", 1, 1, 2),
]
NT = (((1,), (1,)), ((), ()))
NN = (((1,), (0,)), ((), ()))
TN = (((0,), (0,)), ((), ()))


def split(v):
    hi = v.astype(BF16)
    return hi, (v - hi.astype(F32)).astype(BF16)


def dot2(stacked, w, dims):
    both = lax.dot_general(stacked, w, dims, preferred_element_type=F32)
    return both[:ROWS] + both[ROWS:]


def stack(v):
    return jnp.concatenate(split(v), axis=0)


def outer3(a, b):
    ah, al = split(a)
    bh, bl = split(b)
    return lax.dot_general(
        jnp.concatenate([ah, ah, al], axis=0),
        jnp.concatenate([bh, bl, bh], axis=0),
        TN,
        preferred_element_type=F32,
    )


def mean(v):
    return jnp.mean(v, axis=-1, keepdims=True)


def norm(v):
    c = v - mean(v)
    r = lax.rsqrt(mean(c * c) + 1e-05)
    return c * r, r


def norm_back(dy, y, r):
    return r * (dy - mean(dy) - y * mean(dy * y))


def place(ref, v):
    for h in range(2):
        for r in range(2):
            ref[2 * h + r] = v[r * PART : (r + 1) * PART, h * 128 : (h + 1) * 128]


def whole(ref):
    return jnp.concatenate(
        [jnp.concatenate([ref[2 * h], ref[2 * h + 1]], axis=0) for h in range(2)], axis=1
    )


class Place:
    def __init__(self):
        dp, tile = lax.axis_index("dp"), lax.axis_index("tile")
        self.tile = tile
        self.c = lax.rem(dp, 2)
        self.x = lax.rem(dp // 2, X)
        self.zl = dp // (2 * X)
        self.y = lax.rem(tile, Y)
        self.zh = tile // Y

    def at(self, dx=0, dy=0, dzl=0, dzh=0, dc=0):
        x = lax.rem(self.x + dx, X)
        y = lax.rem(self.y + dy, Y)
        zl = lax.rem(self.zl + dzl, ZL)
        zh = lax.rem(self.zh + dzh, ZH)
        c = lax.rem(self.c + dc, 2)
        return ((zl * X + x) * 2 + c, zh * Y + y)


class Sems:
    def __init__(self, send, recv):
        self.send, self.recv, self.n = send, recv, 0

    def copy(self, src, dst, device, send=None, recv=None):
        i = self.n
        self.n += 1
        return pltpu.make_async_remote_copy(
            src_ref=src,
            dst_ref=dst,
            send_sem=self.send.at[i] if send is None else send,
            recv_sem=self.recv.at[i] if recv is None else recv,
            device_id=device,
            device_id_type=MESH,
        )


class TileSum:
    def __init__(self, me, sems, mine, got, pair, total):
        self.me, self.sems = me, sems
        self.mine, self.got, self.pair, self.total = mine, got, pair, total
        self.all = []

    def start(self, copies):
        for c in copies:
            c.start()
        self.all += copies
        return copies

    def scatter(self):
        me = self.me
        self.a = self.start(
            [
                self.sems.copy(self.mine.at[lax.rem(me.y + d, Y)], self.got.at[d - 1], me.at(dy=d))
                for d in (1, 2, 3)
            ]
        )

    def exchange(self):
        for c in self.a:
            c.wait_recv()
        me = self.me
        self.pair[0] = (self.mine[me.y] + self.got[0]) + (self.got[1] + self.got[2])
        self.b = self.start([self.sems.copy(self.pair.at[0], self.pair.at[1], me.at(dzh=1))])

    def gather(self):
        self.b[0].wait_recv()
        me = self.me
        self.total[me.y] = self.pair[0] + self.pair[1]
        here = self.total.at[me.y]
        self.d = self.start([self.sems.copy(here, here, me.at(dy=d)) for d in (1, 2, 3)])

    def result(self):
        for c in self.d:
            c.wait_recv()
        return whole(self.total)

    def close(self):
        for c in self.all:
            c.wait_send()


def section(
    scale,
    feat_in,
    kern_in,
    cot_in,
    wfg_in,
    wval_in,
    wup_in,
    wdown_in,
    gathered,
    gf_out,
    gk_out,
    feat,
    cot,
    kern_v,
    prob,
    prob_b,
    dlog,
    wfg,
    wval,
    wup,
    wdown,
    acc,
    acc2,
    hid,
    slope,
    dhid,
    tmp,
    sums,
    got,
    pair,
    total,
    terms,
    r0,
    mine,
    r1,
    half,
    r2,
    small,
    local,
    send,
    recv,
    shared,
):
    me = Place()
    sems = Sems(send, recv)
    n = kern_in.shape[0]
    cells = feat_in.shape[0]
    chunks = cells // CHUNK
    ff = wup_in.shape[1] // 256
    c, x, y, zl, zh = me.c, me.x, me.y, me.zl, me.zh

    def part(i):
        return pl.ds(pl.multiple_of(i * CHUNK, CHUNK), CHUNK)

    def feat_copy(i):
        return pltpu.make_async_copy(feat_in.at[part(i), :], feat.at[part(i), :], local.at[i])

    def cot_copy(i):
        return pltpu.make_async_copy(cot_in.at[:, part(i)], cot.at[:, part(i)], local.at[chunks + i])

    kern_copy = pltpu.make_async_copy(kern_in, kern_v, local.at[2 * chunks + 4])
    kern_copy.start()
    for i in range(chunks):
        feat_copy(i).start()
    for i in range(chunks):
        cot_copy(i).start()
    base = 2 * chunks
    weights = [
        pltpu.make_async_copy(a, b, local.at[base + i])
        for i, (a, b) in enumerate(((wfg_in, wfg), (wval_in, wval), (wup_in, wup), (wdown_in, wdown)))
    ]
    for w in weights:
        w.start()

    partners = [me.at(dc=1)]
    partners += [me.at(dy=d) for d in (1, 2, 3)]
    partners += [me.at(dx=d) for d in (1, 2, 3)]
    partners += [me.at(dzl=d % ZL, dzh=d // ZL) for d in range(1, ZL * ZH)]
    barrier = pltpu.get_barrier_semaphore()
    for p in partners:
        pl.semaphore_signal(barrier, inc=1, device_id=p, device_id_type=MESH)

    kern_copy.wait()
    kern = kern_v[...]

    acc[...] = jnp.zeros_like(acc)

    def pool(i, carry):
        feat_copy(i).wait()
        f = feat[part(i), :]
        p = jax.nn.sigmoid(lax.dot_general(kern, f, NT, preferred_element_type=F32))
        prob[:, part(i)] = p
        pb = p.astype(BF16)
        prob_b[:, part(i)] = pb
        acc[:n, :] += jnp.dot(pb, f, preferred_element_type=F32)
        return carry

    lax.fori_loop(0, chunks, pool, 0)
    sum_p = TileSum(me, sems, sums.at[0], got.at[0], pair.at[0], total.at[0])
    sum_d = TileSum(me, sems, sums.at[1], got.at[1], pair.at[1], total.at[1])
    sum_m = TileSum(me, sems, sums.at[2], got.at[2], pair.at[2], total.at[2])
    place(sums.at[0], acc[...])
    pl.semaphore_wait(barrier, len(partners))
    sum_p.scatter()

    acc[...] = jnp.zeros_like(acc)

    def new(i, carry):
        cot_copy(i).wait()
        acc[:n, :] += jnp.dot(cot[:, part(i)], feat[part(i), :], preferred_element_type=F32)
        return carry

    lax.fori_loop(0, chunks, new, 0)
    place(sums.at[1], acc[...])
    sum_d.scatter()
    sum_p.exchange()
    sum_d.exchange()
    for w in weights:
        w.wait()
    acc[...] = jnp.zeros_like(acc)
    acc[:n, :] = kern.astype(F32)
    kern32 = acc[...]
    sum_p.gather()
    sum_d.gather()

    pooled = sum_p.result() * scale
    pooled2 = stack(pooled)
    gate = jax.nn.sigmoid(dot2(pooled2, wfg[...], NN))
    value = dot2(pooled2, wval[...], NN)
    k1, rs1 = norm(gate * value + kern32)
    k1s = stack(k1)
    z = k1
    for j in range(ff):
        a = dot2(k1s, wup[:, j * 256 : (j + 1) * 256], NN)
        t = jnp.tanh(0.7978845608028654 * (a + 0.044715 * (a * a * a)))
        up = 0.5 * (1.0 + t)
        h = a * up
        hid[j] = h
        slope[j] = up + 0.5 * a * (1.0 - t * t) * (0.7978845608028654 * (1.0 + 0.134145 * (a * a)))
        z = z + dot2(stack(h), wdown[j * 256 : (j + 1) * 256, :], NN)
    k3, rs3 = norm(z)
    newk = k3.astype(BF16)[:n]

    def slice_of(k, ref):
        first, size = PARTS[k]
        return ref.at[..., pl.ds(first, size), :]

    def spread(first, size, v):
        for h in range(2):
            for i in range(X):
                terms[h, i, first : first + size, :] = v(i)[:, h * 128 : (h + 1) * 128]

    def to_other_core(k):
        cp = sems.copy(slice_of(k, terms.at[1 - c]), slice_of(k, r0), me.at(dc=1))
        cp.start()
        return cp

    dz = norm_back(sum_d.result(), k3, rs3)
    down_term = outer3(hid[me.tile], dz)
    spread(0, 64, lambda i: down_term[i * 64 : (i + 1) * 64])
    c0 = [to_other_core(0)]
    dzs = stack(dz)
    dk1 = dz
    for j in range(ff):
        da = dot2(dzs, wdown[j * 256 : (j + 1) * 256, :], NT) * slope[j]
        dhid[j] = da
        dk1 = dk1 + dot2(stack(da), wup[:, j * 256 : (j + 1) * 256], NT)
    du = norm_back(dk1, k1, rs1)
    dgate = du * value * (gate * (1.0 - gate))
    dvalue = du * gate
    up_term = outer3(k1, dhid[me.tile])
    spread(64, 64, lambda i: up_term[i * 64 : (i + 1) * 64])
    tmp[0] = outer3(pooled, dgate)
    tmp[1] = outer3(pooled, dvalue)

    def own(i):
        return pl.ds(pl.multiple_of(me.tile * 32 + i * 8, 8), 8)

    spread(128, 8, lambda i: tmp[0, own(i), :])
    spread(136, 8, lambda i: tmp[1, own(i), :])
    c0.append(to_other_core(1))

    def across_x(k):
        c0[k].wait_recv()
        first, size = PARTS[k]
        rows = slice(first, first + size)
        mine[:, rows, :] = terms[c, :, rows, :] + r0[:, rows, :]
        cps = [
            sems.copy(slice_of(k, mine.at[lax.rem(x + d, X)]), slice_of(k, r1.at[d - 1]), me.at(dx=d))
            for d in (1, 3, 2)
        ]
        for cp in cps:
            cp.start()
        return cps

    c1 = [across_x(0)]
    dpooled = dot2(stack(dgate), wfg[...], NT) + dot2(stack(dvalue), wval[...], NT)
    dscaled = (dpooled * scale).astype(BF16)
    acc[...] = du

    ds = dscaled[:n]

    def mask(i, carry):
        f = feat[part(i), :]
        p = prob[:, part(i)]
        dp = lax.dot_general(ds, f, NT, preferred_element_type=F32)
        dl = (dp * p * (1.0 - p)).astype(BF16)
        dlog[:, part(i)] = dl
        return carry + jnp.dot(dl, f, preferred_element_type=F32)

    def term(a, b):
        return lax.dot_general(a, b, TN, preferred_element_type=F32)

    def features(i):
        gf_out[part(i), :] = (
            term(cot[:, part(i)], newk) + term(prob_b[:, part(i)], ds) + term(dlog[:, part(i)], kern)
        )

    def piece(k, i):
        return pl.ds(pl.multiple_of(PARTS[k][0] + i * PIECE, PIECE), PIECE)

    tail = pl.ds(*SMALL)

    def across_z(k):
        for cp in c1[k]:
            cp.wait_recv()
        rows = slice(PARTS[k][0], sum(PARTS[k]))
        half[rows, :] = (mine[x, rows, :] + r1[0, rows, :]) + (r1[1, rows, :] + r1[2, rows, :])
        cps = [
            sems.copy(half.at[piece(k, lax.rem(zl + d, ZL)), :], r2.at[d - 1, k], me.at(dzl=d))
            for d in (1, 3, 2)
        ]
        if k == 1:
            small[zl] = half[tail, :]
            cps += [sems.copy(half.at[tail, :], small.at[zl], me.at(dzl=d)) for d in (1, 3, 2)]
        for cp in cps:
            cp.start()
        return cps

    def along_z(k):
        for cp in c2[k]:
            cp.wait_recv()
        gathered[c, zh, y, x, piece(k, zl), :] = (half[piece(k, zl), :] + r2[0, k]) + (r2[1, k] + r2[2, k])
        here = gathered.at[c, zh, y, x, piece(k, zl), :]
        near = [sems.copy(here, here, me.at(dzl=d)) for d in (1, 3, 2)]
        far = [sems.copy(here, here, me.at(dzl=d, dzh=1)) for d in (0, 1, 3, 2)]
        if k == 1:
            gathered[c, zh, y, x, tail, :] = (small[0] + small[1]) + (small[2] + small[3])
            here = gathered.at[c, zh, y, x, tail, :]
            far.append(sems.copy(here, here, me.at(dzh=1)))
        for cp in near + far:
            cp.start()
        return near, far

    mids, lasts, relays = {}, {}, {}

    def axes(q):
        my = lax.rem(zh + q, ZH)
        return 1 - my, my

    def block(q, m, l):
        mx, my = axes(q)
        bx = lax.rem(x + mx * m + my * l, X)
        by = lax.rem(y + my * m + mx * l, Y)
        return gathered.at[c, lax.rem(zh + q, ZH), by, bx]

    def send_to(b, device):
        cp = sems.copy(b, b, device, send=shared.at[0])
        cp.start()
        return cp

    def to_twin(b):
        sems.copy(b, b, me.at(dc=1), send=shared.at[1], recv=shared.at[2]).start()

    def along_mid(q, d):
        mx, my = axes(q)
        return me.at(dx=mx * d, dy=my * d)

    def along_last(q, d):
        mx, my = axes(q)
        return me.at(dx=my * d, dy=mx * d)

    def have(k, *spot):
        to_twin(slice_of(k, block(*spot)))

    def open_mid(k, q):
        for cp in zs[k][q]:
            cp.wait_recv()
        b = slice_of(k, block(q, 0, 0))
        for d in (1, 3, 2):
            mids[k, q, d] = send_to(b, along_mid(q, d))
        open_last(k, q, 0)

    def open_last(k, q, m):
        if m:
            mids[k, q, m].wait_recv()
        b = slice_of(k, block(q, (4 - m) % 4, 0))
        lasts[k, q, m] = {d: send_to(b, along_last(q, d)) for d in (1, 3)}
        have(k, q, (4 - m) % 4, 0)

    def relay(k, q, m):
        relays[k, q, m] = []
        size = PARTS[k][1] // 2
        for d, first in ((1, PARTS[k][0]), (3, PARTS[k][0] + size)):
            lasts[k, q, m][d].wait_recv()
            b = block(q, (4 - m) % 4, 4 - d).at[pl.ds(first, size), :]
            relays[k, q, m].append(send_to(b, along_last(q, d)))
            have(k, q, (4 - m) % 4, 4 - d)

    def close(k, q, m):
        for cp in relays[k, q, m]:
            cp.wait_recv()
        have(k, q, (4 - m) % 4, 2)

    c1.append(across_x(1))
    macc = lax.fori_loop(0, 3, mask, jnp.zeros((n, 256), F32))
    c2 = [across_z(0)]
    macc = lax.fori_loop(3, chunks, mask, macc)
    acc2[...] = jnp.zeros_like(acc2)
    acc2[:n, :] = macc
    place(sums.at[2], acc2[...])
    sum_m.scatter()
    c2.append(across_z(1))
    features(0)
    zs = [along_z(0)]
    sum_m.exchange()
    features(1)
    zs.append(along_z(1))
    features(2)
    open_mid(0, 0)
    features(3)
    open_mid(0, 1)
    open_mid(1, 0)
    sum_m.gather()
    features(4)
    rest = {"l": open_last, "r": relay, "c": close}
    for step, k, q, m in ORDER:
        if step == "m":
            open_mid(k, q)
        else:
            rest[step](k, q, m)
    gk_out[:, 0, :] = (sum_m.result() + acc[...])[:n]
    half_of_all = gathered.at[0]
    for i in (2, 1):
        pltpu.make_async_copy(half_of_all, half_of_all, shared.at[i]).wait()
    for sent in (gathered.at[0, 0], gathered.at[0, 1, pl.ds(0, 3)], gathered.at[1, 0, 0, pl.ds(0, 2)]):
        pltpu.make_async_copy(sent, sent, shared.at[0]).wait()

    for s in (sum_p, sum_d, sum_m):
        s.close()
    for k in range(2):
        for cp in [c0[k]] + c1[k] + c2[k] + zs[k][0] + zs[k][1]:
            cp.wait_send()


def finish(gathered, gf, gk, grad_f, grad_k, g_gate, g_value, g_up, g_down, sem):
    pairs = [(gf, grad_f), (gk, grad_k)]
    for h in range(2):
        lanes = pl.ds(h * 128, 128)
        for t in range(ZH * Y):
            src = gathered.at[h, t // Y, t % Y]
            pairs += [
                (src.at[:, 0:64, :], g_down.at[t, :, :, lanes]),
                (src.at[:, 64:128, :], g_up.at[:, :, pl.ds(t * 256 + h * 128, 128)]),
                (src.at[:, 128:136, :], g_gate.at[t, :, :, lanes]),
                (src.at[:, 136:144, :], g_value.at[t, :, :, lanes]),
            ]
    copies = [pltpu.make_async_copy(a, b, sem.at[i]) for i, (a, b) in enumerate(pairs)]
    for cp in copies:
        cp.start()
    for cp in copies:
        cp.wait()


def shards(features, kernels, cotangent, w_feat_gate, w_value, w_up, w_down):
    feat, kern, cot = features[0], kernels[0], cotangent[0]
    n, channels = kern.shape
    cells = feat.shape[0]
    chunks = cells // CHUNK
    ff = w_up.shape[1] // 256
    scale = 1.0 / math.sqrt(lax.axis_size("tile") * cells)
    anywhere = pl.BlockSpec(memory_space=pl.ANY)

    def hbm(v):
        return pltpu.with_memory_space_constraint(v, pltpu.HBM)

    def vmem_array(v):
        return pltpu.with_memory_space_constraint(v, pltpu.VMEM)

    vmem = pl.BlockSpec(memory_space=pltpu.VMEM)
    copies = 200
    shape = jax.ShapeDtypeStruct
    gathered, gf, gk = pl.pallas_call(
        functools.partial(section, scale),
        out_shape=(
            shape((2, ZH, Y, X, BLOCK, 128), F32),
            shape((cells, channels), F32),
            shape((n, 1, channels), F32),
        ),
        in_specs=[anywhere] * 7,
        out_specs=(vmem, vmem, vmem),
        scratch_shapes=[
            pltpu.VMEM((cells, channels), BF16),
            pltpu.VMEM((n, cells), BF16),
            pltpu.VMEM((n, channels), BF16),
            pltpu.VMEM((n, cells), F32),
            pltpu.VMEM((n, cells), BF16),
            pltpu.VMEM((n, cells), BF16),
            pltpu.VMEM(w_feat_gate.shape, BF16),
            pltpu.VMEM(w_value.shape, BF16),
            pltpu.VMEM(w_up.shape, BF16),
            pltpu.VMEM(w_down.shape, BF16),
            pltpu.VMEM((ROWS, channels), F32),
            pltpu.VMEM((ROWS, channels), F32),
            pltpu.VMEM((ff, ROWS, 256), F32),
            pltpu.VMEM((ff, ROWS, 256), F32),
            pltpu.VMEM((ff, ROWS, 256), F32),
            pltpu.VMEM((2, 256, 256), F32),
            pltpu.VMEM((3, 4, PART, 128), F32),
            pltpu.VMEM((3, 3, PART, 128), F32),
            pltpu.VMEM((3, 2, PART, 128), F32),
            pltpu.VMEM((3, 4, PART, 128), F32),
            pltpu.VMEM((2, X, BLOCK, 128), F32),
            pltpu.VMEM((X, BLOCK, 128), F32),
            pltpu.VMEM((X, BLOCK, 128), F32),
            pltpu.VMEM((3, BLOCK, 128), F32),
            pltpu.VMEM((BLOCK, 128), F32),
            pltpu.VMEM((3, 2, PIECE, 128), F32),
            pltpu.VMEM((ZL, SMALL[1], 128), F32),
            pltpu.SemaphoreType.DMA((2 * chunks + 5,)),
            pltpu.SemaphoreType.DMA((copies,)),
            pltpu.SemaphoreType.DMA((copies,)),
            pltpu.SemaphoreType.DMA((3,)),
        ],
        compiler_params=pltpu.CompilerParams(
            collective_id=0, has_side_effects=True, vmem_limit_bytes=32 * 2**20
        ),
        name="section",
    )(hbm(feat), hbm(kern), hbm(cot), hbm(w_feat_gate), hbm(w_value), hbm(w_up), hbm(w_down))

    tiles = ZH * Y
    grad_f, grad_k, g_gate, g_value, g_up, g_down = pl.pallas_call(
        finish,
        out_shape=(
            shape((cells, channels), F32),
            shape((n, 1, channels), F32),
            shape((tiles, X, 8, channels), F32),
            shape((tiles, X, 8, channels), F32),
            shape((X, 64, w_up.shape[1]), F32),
            shape((tiles, X, 64, channels), F32),
        ),
        in_specs=[vmem] * 3,
        out_specs=(anywhere,) * 6,
        scratch_shapes=[pltpu.SemaphoreType.DMA((2 + tiles * 2 * 4,))],
        compiler_params=pltpu.CompilerParams(vmem_limit_bytes=2**20),
        name="finish",
    )(vmem_array(gathered), vmem_array(gf), vmem_array(gk))
    return (
        grad_f[None],
        jnp.transpose(grad_k, (1, 0, 2)),
        g_gate.reshape(w_feat_gate.shape),
        g_value.reshape(w_value.shape),
        g_up.reshape(w_up.shape),
        g_down.reshape(w_down.shape),
    )


def solution(mesh):
    placed = (P("dp", "tile", None), P("dp", None, None), P("dp", None, "tile"), P(), P(), P(), P())
    return jax.shard_map(
        shards,
        mesh=mesh,
        in_specs=placed,
        out_specs=(P("dp", "tile", None), P("dp", None, None), P(), P(), P(), P()),
        check_vma=False,
    )
```

```python
import functools
import math

import jax
import jax.numpy as jnp
from jax import lax
from jax.experimental import pallas as pl
from jax.experimental.pallas import tpu as pltpu
from jax.sharding import PartitionSpec as P

MESH = pl.DeviceIdType.MESH
F32, BF16 = jnp.float32, jnp.bfloat16
X, Y, ZL, ZH = 4, 4, 4, 2
ROWS = 112
PART = 56
CHUNK = 1024
PIECE = 16
BLOCK = 144
PARTS = ((0, 64), (64, 80))
SMALL = (128, 16)
ORDER = [
    ("l", 0, 0, 1),
    ("l", 0, 0, 3),
    ("r", 0, 0, 0),
    ("l", 0, 0, 2),
    ("m", 1, 1, 0),
    ("l", 0, 1, 1),
    ("l", 0, 1, 3),
    ("r", 0, 1, 0),
    ("l", 1, 0, 1),
    ("l", 1, 0, 3),
    ("l", 0, 1, 2),
    ("r", 1, 0, 0),
    ("r", 0, 0, 1),
    ("l", 1, 0, 2),
    ("r", 1, 1, 0),
    ("r", 0, 0, 3),
    ("c", 0, 0, 0),
    ("r", 0, 1, 1),
    ("r", 0, 0, 2),
    ("r", 0, 1, 3),
    ("c", 0, 1, 0),
    ("l", 1, 1, 1),
    ("l", 1, 1, 3),
    ("r", 0, 1, 2),
    ("c", 1, 1, 0),
    ("c", 0, 1, 1),
    ("c", 0, 1, 3),
    ("l", 1, 1, 2),
    ("r", 1, 0, 1),
    ("r", 1, 0, 3),
    ("r", 1, 1, 1),
    ("c", 1, 0, 0),
    ("c", 0, 0, 1),
    ("r", 1, 1, 3),
    ("c", 0, 1, 2),
    ("r", 1, 0, 2),
    ("c", 0, 0, 3),
    ("r", 1, 1, 2),
    ("c", 0, 0, 2),
    ("c", 1, 1, 1),
    ("c", 1, 0, 1),
    ("c", 1, 0, 3),
    ("c", 1, 1, 3),
    ("c", 1, 0, 2),
    ("c", 1, 1, 2),
]
NT = (((1,), (1,)), ((), ()))
NN = (((1,), (0,)), ((), ()))
TN = (((0,), (0,)), ((), ()))


def split(v):
    hi = v.astype(BF16)
    return hi, (v - hi.astype(F32)).astype(BF16)


def dot2(stacked, w, dims):
    both = lax.dot_general(stacked, w, dims, preferred_element_type=F32)
    return both[:ROWS] + both[ROWS:]


def stack(v):
    return jnp.concatenate(split(v), axis=0)


def outer3(a, b):
    ah, al = split(a)
    bh, bl = split(b)
    return lax.dot_general(
        jnp.concatenate([ah, ah, al], axis=0),
        jnp.concatenate([bh, bl, bh], axis=0),
        TN,
        preferred_element_type=F32,
    )


def mean(v):
    return jnp.mean(v, axis=-1, keepdims=True)


def norm(v):
    c = v - mean(v)
    r = lax.rsqrt(mean(c * c) + 1e-05)
    return c * r, r


def norm_back(dy, y, r):
    return r * (dy - mean(dy) - y * mean(dy * y))


def place(ref, v):
    for h in range(2):
        for r in range(2):
            ref[2 * h + r] = v[r * PART : (r + 1) * PART, h * 128 : (h + 1) * 128]


def whole(ref):
    return jnp.concatenate(
        [jnp.concatenate([ref[2 * h], ref[2 * h + 1]], axis=0) for h in range(2)], axis=1
    )


class Place:
    def __init__(self):
        dp, tile = lax.axis_index("dp"), lax.axis_index("tile")
        self.tile = tile
        self.c = lax.rem(dp, 2)
        self.x = lax.rem(dp // 2, X)
        self.zl = dp // (2 * X)
        self.y = lax.rem(tile, Y)
        self.zh = tile // Y

    def at(self, dx=0, dy=0, dzl=0, dzh=0, dc=0):
        x = lax.rem(self.x + dx, X)
        y = lax.rem(self.y + dy, Y)
        zl = lax.rem(self.zl + dzl, ZL)
        zh = lax.rem(self.zh + dzh, ZH)
        c = lax.rem(self.c + dc, 2)
        return ((zl * X + x) * 2 + c, zh * Y + y)


class Sems:
    def __init__(self, send, recv):
        self.send, self.recv, self.n = send, recv, 0

    def copy(self, src, dst, device, send=None, recv=None):
        i = self.n
        self.n += 1
        return pltpu.make_async_remote_copy(
            src_ref=src,
            dst_ref=dst,
            send_sem=self.send.at[i] if send is None else send,
            recv_sem=self.recv.at[i] if recv is None else recv,
            device_id=device,
            device_id_type=MESH,
        )


class TileSum:
    def __init__(self, me, sems, mine, got, pair, total):
        self.me, self.sems = me, sems
        self.mine, self.got, self.pair, self.total = mine, got, pair, total
        self.all = []

    def start(self, copies):
        for c in copies:
            c.start()
        self.all += copies
        return copies

    def scatter(self):
        me = self.me
        self.a = self.start(
            [
                self.sems.copy(self.mine.at[lax.rem(me.y + d, Y)], self.got.at[d - 1], me.at(dy=d))
                for d in (1, 2, 3)
            ]
        )

    def exchange(self):
        for c in self.a:
            c.wait_recv()
        me = self.me
        self.pair[0] = (self.mine[me.y] + self.got[0]) + (self.got[1] + self.got[2])
        self.b = self.start([self.sems.copy(self.pair.at[0], self.pair.at[1], me.at(dzh=1))])

    def gather(self):
        self.b[0].wait_recv()
        me = self.me
        self.total[me.y] = self.pair[0] + self.pair[1]
        here = self.total.at[me.y]
        self.d = self.start([self.sems.copy(here, here, me.at(dy=d)) for d in (1, 2, 3)])

    def result(self):
        for c in self.d:
            c.wait_recv()
        return whole(self.total)

    def close(self):
        for c in self.all:
            c.wait_send()


def section(
    scale,
    feat_in,
    kern_in,
    cot_in,
    wfg_in,
    wval_in,
    wup_in,
    wdown_in,
    gathered,
    gf_out,
    gk_out,
    feat,
    cot,
    kern_v,
    prob,
    prob_b,
    dlog,
    wfg,
    wval,
    wup,
    wdown,
    acc,
    acc2,
    hid,
    slope,
    dhid,
    tmp,
    sums,
    got,
    pair,
    total,
    terms,
    r0,
    mine,
    r1,
    half,
    r2,
    small,
    local,
    send,
    recv,
    shared,
):
    me = Place()
    sems = Sems(send, recv)
    n = kern_in.shape[0]
    cells = feat_in.shape[0]
    chunks = cells // CHUNK
    ff = wup_in.shape[1] // 256
    c, x, y, zl, zh = me.c, me.x, me.y, me.zl, me.zh

    def part(i):
        return pl.ds(pl.multiple_of(i * CHUNK, CHUNK), CHUNK)

    def feat_copy(i):
        return pltpu.make_async_copy(feat_in.at[part(i), :], feat.at[part(i), :], local.at[i])

    def cot_copy(i):
        return pltpu.make_async_copy(cot_in.at[:, part(i)], cot.at[:, part(i)], local.at[chunks + i])

    kern_copy = pltpu.make_async_copy(kern_in, kern_v, local.at[2 * chunks + 4])
    kern_copy.start()
    for i in range(chunks):
        feat_copy(i).start()
    for i in range(chunks):
        cot_copy(i).start()
    base = 2 * chunks
    weights = [
        pltpu.make_async_copy(a, b, local.at[base + i])
        for i, (a, b) in enumerate(((wfg_in, wfg), (wval_in, wval), (wup_in, wup), (wdown_in, wdown)))
    ]
    for w in weights:
        w.start()

    partners = [me.at(dc=1)]
    partners += [me.at(dy=d) for d in (1, 2, 3)]
    partners += [me.at(dx=d) for d in (1, 2, 3)]
    partners += [me.at(dzl=d % ZL, dzh=d // ZL) for d in range(1, ZL * ZH)]
    barrier = pltpu.get_barrier_semaphore()
    for p in partners:
        pl.semaphore_signal(barrier, inc=1, device_id=p, device_id_type=MESH)

    kern_copy.wait()
    kern = kern_v[...]

    acc[...] = jnp.zeros_like(acc)

    def pool(i, carry):
        feat_copy(i).wait()
        f = feat[part(i), :]
        p = jax.nn.sigmoid(lax.dot_general(kern, f, NT, preferred_element_type=F32))
        prob[:, part(i)] = p
        pb = p.astype(BF16)
        prob_b[:, part(i)] = pb
        acc[:n, :] += jnp.dot(pb, f, preferred_element_type=F32)
        return carry

    lax.fori_loop(0, chunks, pool, 0)
    sum_p = TileSum(me, sems, sums.at[0], got.at[0], pair.at[0], total.at[0])
    sum_d = TileSum(me, sems, sums.at[1], got.at[1], pair.at[1], total.at[1])
    sum_m = TileSum(me, sems, sums.at[2], got.at[2], pair.at[2], total.at[2])
    place(sums.at[0], acc[...])
    pl.semaphore_wait(barrier, len(partners))
    sum_p.scatter()

    acc[...] = jnp.zeros_like(acc)

    def new(i, carry):
        cot_copy(i).wait()
        acc[:n, :] += jnp.dot(cot[:, part(i)], feat[part(i), :], preferred_element_type=F32)
        return carry

    lax.fori_loop(0, chunks, new, 0)
    place(sums.at[1], acc[...])
    sum_d.scatter()
    sum_p.exchange()
    sum_d.exchange()
    for w in weights:
        w.wait()
    acc[...] = jnp.zeros_like(acc)
    acc[:n, :] = kern.astype(F32)
    kern32 = acc[...]
    sum_p.gather()
    sum_d.gather()

    pooled = sum_p.result() * scale
    pooled2 = stack(pooled)
    gate = jax.nn.sigmoid(dot2(pooled2, wfg[...], NN))
    value = dot2(pooled2, wval[...], NN)
    k1, rs1 = norm(gate * value + kern32)
    k1s = stack(k1)
    z = k1
    for j in range(ff):
        a = dot2(k1s, wup[:, j * 256 : (j + 1) * 256], NN)
        t = jnp.tanh(0.7978845608028654 * (a + 0.044715 * (a * a * a)))
        up = 0.5 * (1.0 + t)
        h = a * up
        hid[j] = h
        slope[j] = up + 0.5 * a * (1.0 - t * t) * (0.7978845608028654 * (1.0 + 0.134145 * (a * a)))
        z = z + dot2(stack(h), wdown[j * 256 : (j + 1) * 256, :], NN)
    k3, rs3 = norm(z)
    newk = k3.astype(BF16)[:n]

    def slice_of(k, ref):
        first, size = PARTS[k]
        return ref.at[..., pl.ds(first, size), :]

    def spread(first, size, v):
        for h in range(2):
            for i in range(X):
                terms[h, i, first : first + size, :] = v(i)[:, h * 128 : (h + 1) * 128]

    def to_other_core(k):
        cp = sems.copy(slice_of(k, terms.at[1 - c]), slice_of(k, r0), me.at(dc=1))
        cp.start()
        return cp

    dz = norm_back(sum_d.result(), k3, rs3)
    down_term = outer3(hid[me.tile], dz)
    spread(0, 64, lambda i: down_term[i * 64 : (i + 1) * 64])
    c0 = [to_other_core(0)]
    dzs = stack(dz)
    dk1 = dz
    for j in range(ff):
        da = dot2(dzs, wdown[j * 256 : (j + 1) * 256, :], NT) * slope[j]
        dhid[j] = da
        dk1 = dk1 + dot2(stack(da), wup[:, j * 256 : (j + 1) * 256], NT)
    def across_x(k):
        c0[k].wait_recv()
        first, size = PARTS[k]
        rows = slice(first, first + size)
        mine[:, rows, :] = terms[c, :, rows, :] + r0[:, rows, :]
        cps = [
            sems.copy(slice_of(k, mine.at[lax.rem(x + d, X)]), slice_of(k, r1.at[d - 1]), me.at(dx=d))
            for d in (1, 3, 2)
        ]
        for cp in cps:
            cp.start()
        return cps

    c1 = [across_x(0)]
    du = norm_back(dk1, k1, rs1)
    dgate = du * value * (gate * (1.0 - gate))
    dvalue = du * gate
    up_term = outer3(k1, dhid[me.tile])
    spread(64, 64, lambda i: up_term[i * 64 : (i + 1) * 64])
    tmp[0] = outer3(pooled, dgate)
    tmp[1] = outer3(pooled, dvalue)

    def own(i):
        return pl.ds(pl.multiple_of(me.tile * 32 + i * 8, 8), 8)

    spread(128, 8, lambda i: tmp[0, own(i), :])
    spread(136, 8, lambda i: tmp[1, own(i), :])
    c0.append(to_other_core(1))

    dpooled = dot2(stack(dgate), wfg[...], NT) + dot2(stack(dvalue), wval[...], NT)
    dscaled = (dpooled * scale).astype(BF16)
    acc[...] = du

    ds = dscaled[:n]

    def mask(i, carry):
        f = feat[part(i), :]
        p = prob[:, part(i)]
        dp = lax.dot_general(ds, f, NT, preferred_element_type=F32)
        dl = (dp * p * (1.0 - p)).astype(BF16)
        dlog[:, part(i)] = dl
        return carry + jnp.dot(dl, f, preferred_element_type=F32)

    def term(a, b):
        return lax.dot_general(a, b, TN, preferred_element_type=F32)

    def features(i):
        gf_out[part(i), :] = (
            term(cot[:, part(i)], newk) + term(prob_b[:, part(i)], ds) + term(dlog[:, part(i)], kern)
        )

    def piece(k, i):
        return pl.ds(pl.multiple_of(PARTS[k][0] + i * PIECE, PIECE), PIECE)

    tail = pl.ds(*SMALL)

    def across_z(k):
        for cp in c1[k]:
            cp.wait_recv()
        rows = slice(PARTS[k][0], sum(PARTS[k]))
        half[rows, :] = (mine[x, rows, :] + r1[0, rows, :]) + (r1[1, rows, :] + r1[2, rows, :])
        cps = [
            sems.copy(half.at[piece(k, lax.rem(zl + d, ZL)), :], r2.at[d - 1, k], me.at(dzl=d))
            for d in (1, 3, 2)
        ]
        if k == 1:
            small[zl] = half[tail, :]
            cps += [sems.copy(half.at[tail, :], small.at[zl], me.at(dzl=d)) for d in (1, 3, 2)]
        for cp in cps:
            cp.start()
        return cps

    def along_z(k):
        for cp in c2[k]:
            cp.wait_recv()
        gathered[c, zh, y, x, piece(k, zl), :] = (half[piece(k, zl), :] + r2[0, k]) + (r2[1, k] + r2[2, k])
        here = gathered.at[c, zh, y, x, piece(k, zl), :]
        near = [sems.copy(here, here, me.at(dzl=d)) for d in (1, 3, 2)]
        far = [sems.copy(here, here, me.at(dzl=d, dzh=1)) for d in (0, 1, 3, 2)]
        if k == 1:
            gathered[c, zh, y, x, tail, :] = (small[0] + small[1]) + (small[2] + small[3])
            here = gathered.at[c, zh, y, x, tail, :]
            far.append(sems.copy(here, here, me.at(dzh=1)))
        for cp in near + far:
            cp.start()
        return near, far

    mids, lasts, relays = {}, {}, {}

    def axes(q):
        my = lax.rem(zh + q, ZH)
        return 1 - my, my

    def block(q, m, l):
        mx, my = axes(q)
        bx = lax.rem(x + mx * m + my * l, X)
        by = lax.rem(y + my * m + mx * l, Y)
        return gathered.at[c, lax.rem(zh + q, ZH), by, bx]

    def send_to(b, device):
        cp = sems.copy(b, b, device, send=shared.at[0])
        cp.start()
        return cp

    def to_twin(b):
        sems.copy(b, b, me.at(dc=1), send=shared.at[1], recv=shared.at[2]).start()

    def along_mid(q, d):
        mx, my = axes(q)
        return me.at(dx=mx * d, dy=my * d)

    def along_last(q, d):
        mx, my = axes(q)
        return me.at(dx=my * d, dy=mx * d)

    def have(k, *spot):
        to_twin(slice_of(k, block(*spot)))

    def open_mid(k, q):
        for cp in zs[k][q]:
            cp.wait_recv()
        b = slice_of(k, block(q, 0, 0))
        for d in (1, 3, 2):
            mids[k, q, d] = send_to(b, along_mid(q, d))
        open_last(k, q, 0)

    def open_last(k, q, m):
        if m:
            mids[k, q, m].wait_recv()
        b = slice_of(k, block(q, (4 - m) % 4, 0))
        lasts[k, q, m] = {d: send_to(b, along_last(q, d)) for d in (1, 3)}
        have(k, q, (4 - m) % 4, 0)

    def relay(k, q, m):
        relays[k, q, m] = []
        size = PARTS[k][1] // 2
        for d, first in ((1, PARTS[k][0]), (3, PARTS[k][0] + size)):
            lasts[k, q, m][d].wait_recv()
            b = block(q, (4 - m) % 4, 4 - d).at[pl.ds(first, size), :]
            relays[k, q, m].append(send_to(b, along_last(q, d)))
            have(k, q, (4 - m) % 4, 4 - d)

    def close(k, q, m):
        for cp in relays[k, q, m]:
            cp.wait_recv()
        have(k, q, (4 - m) % 4, 2)

    c1.append(across_x(1))
    macc = lax.fori_loop(0, 2, mask, jnp.zeros((n, 256), F32))
    c2 = [across_z(0)]
    macc = lax.fori_loop(2, 4, mask, macc)
    c2.append(across_z(1))
    macc = lax.fori_loop(4, chunks, mask, macc)
    zs = [along_z(0)]
    acc2[...] = jnp.zeros_like(acc2)
    acc2[:n, :] = macc
    place(sums.at[2], acc2[...])
    sum_m.scatter()
    features(0)
    zs.append(along_z(1))
    sum_m.exchange()
    features(1)
    open_mid(0, 0)
    features(2)
    open_mid(0, 1)
    open_mid(1, 0)
    sum_m.gather()
    features(3)
    features(4)
    rest = {"l": open_last, "r": relay, "c": close}
    for step, k, q, m in ORDER:
        if step == "m":
            open_mid(k, q)
        else:
            rest[step](k, q, m)
    gk_out[:, 0, :] = (sum_m.result() + acc[...])[:n]
    half_of_all = gathered.at[0]
    for i in (2, 1):
        pltpu.make_async_copy(half_of_all, half_of_all, shared.at[i]).wait()
    for sent in (gathered.at[0, 0], gathered.at[0, 1, pl.ds(0, 3)], gathered.at[1, 0, 0, pl.ds(0, 2)]):
        pltpu.make_async_copy(sent, sent, shared.at[0]).wait()

    for s in (sum_p, sum_d, sum_m):
        s.close()
    for k in range(2):
        for cp in [c0[k]] + c1[k] + c2[k] + zs[k][0] + zs[k][1]:
            cp.wait_send()


def finish(gathered, gf, gk, grad_f, grad_k, g_gate, g_value, g_up, g_down, sem):
    pairs = [(gf, grad_f), (gk, grad_k)]
    for h in range(2):
        lanes = pl.ds(h * 128, 128)
        for t in range(ZH * Y):
            src = gathered.at[h, t // Y, t % Y]
            pairs += [
                (src.at[:, 0:64, :], g_down.at[t, :, :, lanes]),
                (src.at[:, 64:128, :], g_up.at[:, :, pl.ds(t * 256 + h * 128, 128)]),
                (src.at[:, 128:136, :], g_gate.at[t, :, :, lanes]),
                (src.at[:, 136:144, :], g_value.at[t, :, :, lanes]),
            ]
    copies = [pltpu.make_async_copy(a, b, sem.at[i]) for i, (a, b) in enumerate(pairs)]
    for cp in copies:
        cp.start()
    for cp in copies:
        cp.wait()


def shards(features, kernels, cotangent, w_feat_gate, w_value, w_up, w_down):
    feat, kern, cot = features[0], kernels[0], cotangent[0]
    n, channels = kern.shape
    cells = feat.shape[0]
    chunks = cells // CHUNK
    ff = w_up.shape[1] // 256
    scale = 1.0 / math.sqrt(lax.axis_size("tile") * cells)
    anywhere = pl.BlockSpec(memory_space=pl.ANY)

    def hbm(v):
        return pltpu.with_memory_space_constraint(v, pltpu.HBM)

    def vmem_array(v):
        return pltpu.with_memory_space_constraint(v, pltpu.VMEM)

    vmem = pl.BlockSpec(memory_space=pltpu.VMEM)
    copies = 200
    shape = jax.ShapeDtypeStruct
    gathered, gf, gk = pl.pallas_call(
        functools.partial(section, scale),
        out_shape=(
            shape((2, ZH, Y, X, BLOCK, 128), F32),
            shape((cells, channels), F32),
            shape((n, 1, channels), F32),
        ),
        in_specs=[anywhere] * 7,
        out_specs=(vmem, vmem, vmem),
        scratch_shapes=[
            pltpu.VMEM((cells, channels), BF16),
            pltpu.VMEM((n, cells), BF16),
            pltpu.VMEM((n, channels), BF16),
            pltpu.VMEM((n, cells), F32),
            pltpu.VMEM((n, cells), BF16),
            pltpu.VMEM((n, cells), BF16),
            pltpu.VMEM(w_feat_gate.shape, BF16),
            pltpu.VMEM(w_value.shape, BF16),
            pltpu.VMEM(w_up.shape, BF16),
            pltpu.VMEM(w_down.shape, BF16),
            pltpu.VMEM((ROWS, channels), F32),
            pltpu.VMEM((ROWS, channels), F32),
            pltpu.VMEM((ff, ROWS, 256), F32),
            pltpu.VMEM((ff, ROWS, 256), F32),
            pltpu.VMEM((ff, ROWS, 256), F32),
            pltpu.VMEM((2, 256, 256), F32),
            pltpu.VMEM((3, 4, PART, 128), F32),
            pltpu.VMEM((3, 3, PART, 128), F32),
            pltpu.VMEM((3, 2, PART, 128), F32),
            pltpu.VMEM((3, 4, PART, 128), F32),
            pltpu.VMEM((2, X, BLOCK, 128), F32),
            pltpu.VMEM((X, BLOCK, 128), F32),
            pltpu.VMEM((X, BLOCK, 128), F32),
            pltpu.VMEM((3, BLOCK, 128), F32),
            pltpu.VMEM((BLOCK, 128), F32),
            pltpu.VMEM((3, 2, PIECE, 128), F32),
            pltpu.VMEM((ZL, SMALL[1], 128), F32),
            pltpu.SemaphoreType.DMA((2 * chunks + 5,)),
            pltpu.SemaphoreType.DMA((copies,)),
            pltpu.SemaphoreType.DMA((copies,)),
            pltpu.SemaphoreType.DMA((3,)),
        ],
        compiler_params=pltpu.CompilerParams(
            collective_id=0, has_side_effects=True, vmem_limit_bytes=32 * 2**20
        ),
        name="section",
    )(hbm(feat), hbm(kern), hbm(cot), hbm(w_feat_gate), hbm(w_value), hbm(w_up), hbm(w_down))

    tiles = ZH * Y
    grad_f, grad_k, g_gate, g_value, g_up, g_down = pl.pallas_call(
        finish,
        out_shape=(
            shape((cells, channels), F32),
            shape((n, 1, channels), F32),
            shape((tiles, X, 8, channels), F32),
            shape((tiles, X, 8, channels), F32),
            shape((X, 64, w_up.shape[1]), F32),
            shape((tiles, X, 64, channels), F32),
        ),
        in_specs=[vmem] * 3,
        out_specs=(anywhere,) * 6,
        scratch_shapes=[pltpu.SemaphoreType.DMA((2 + tiles * 2 * 4,))],
        compiler_params=pltpu.CompilerParams(vmem_limit_bytes=2**20),
        name="finish",
    )(vmem_array(gathered), vmem_array(gf), vmem_array(gk))
    return (
        grad_f[None],
        jnp.transpose(grad_k, (1, 0, 2)),
        g_gate.reshape(w_feat_gate.shape),
        g_value.reshape(w_value.shape),
        g_up.reshape(w_up.shape),
        g_down.reshape(w_down.shape),
    )


def solution(mesh):
    placed = (P("dp", "tile", None), P("dp", None, None), P("dp", None, "tile"), P(), P(), P(), P())
    return jax.shard_map(
        shards,
        mesh=mesh,
        in_specs=placed,
        out_specs=(P("dp", "tile", None), P("dp", None, None), P(), P(), P(), P()),
        check_vma=False,
    )
```
